256 devices in a mesh: sx: 8 (over y, x_hi), sy: 2 (over x_lo), snap: 16 (over z, core).
Axes of the slice: x: 4 (x_hi: 2, x_lo: 2; x = x_hi * 2 + x_lo), y: 4, z: 8, core: 2. Of those that a mesh axis runs over, the one named last changes fastest.
Arguments:
- snapshots: float32 [32, 8, 64, 4096], P('sx', 'sy', None, 'snap'), may hold values from -6 to 6
- links: int32 [32, 8, 9], P('sx', 'sy'), may hold values from 0 to 8, each once within a row
- mass: float32 [32, 8, 9, 4096], P('sx', 'sy'), may hold values from -0.25 to 0.25
Outputs:
- weighted: float32 [32, 8, 64, 4096], P('sx', 'sy', None, 'snap')
- gram: float32 [4096, 4096], P('snap', ('sx', 'sy'))
The draws below stay inside these ranges and needn't reach their ends.
All inputs are finite; a program needn't handle non-finite values.
Results may differ from the reference program's by a relative error of at most 0.0001.
Values sent between devices are 32-bit elements; how exact they have to be, the bound alone decides.
No kernel may reach another device: no remote copies, remote signals or barrier semaphores. Data moves between devices by JAX's collectives and lax.ppermute only.
A program may use at most 128 MiB of HBM per device.

```python
import jax
import jax.numpy as jnp
from jax import lax

BLK = 64
NEIGH = 9
SNAPS = 4096
BX = 32
BY = 8


def levels(own_key, extent, split, low, largest):
    level = 1.0
    for position, parts in split:
        draws = jax.random.uniform(jax.random.fold_in(jax.random.fold_in(own_key, 6), position), (parts,), jnp.float32, low / len(split), largest / len(split))
        level = level * jnp.repeat(jnp.exp(draws), extent[position] // parts).reshape((-1,) + (1,) * (len(extent) - 1 - position))
    return level


def scatter_about(own_key, extent, spread, bound, shards=(), held_as=jnp.bfloat16):
    factor_of = levels(own_key, extent, shards, -0.22, 0.18) if shards else 1.0
    array = jax.random.normal(own_key, extent, jnp.float32) * spread * factor_of
    return jnp.minimum(jnp.maximum(array, -bound), bound).astype(held_as)


def setup_inputs(seed: int = 0) -> dict:
    key_of = jax.random.split(jax.random.key(seed), 4)
    snapshots = scatter_about(key_of[0], (BX, BY, BLK, SNAPS), 1.0, 6.0, ((0, 8), (1, 2), (3, 16)), jnp.float32)
    links = jax.vmap(lambda own: jax.random.permutation(own, NEIGH))(jax.random.split(key_of[1], BX * BY)).reshape((BX, BY, NEIGH)).astype(jnp.int32)
    mass = scatter_about(key_of[2], (BX, BY, NEIGH, BLK * BLK), (NEIGH * BLK) ** -0.5, 0.25, ((0, 8), (1, 2)), jnp.float32)
    return dict(snapshots=snapshots, links=links, mass=mass)


def reference(snapshots, links, mass):
    grid_x, grid_y, block_len, snap_cols = snapshots.shape
    blocks = mass.reshape(grid_x, grid_y, NEIGH, block_len, block_len)
    padded = jnp.pad(snapshots, ((1, 1), (1, 1), (0, 0), (0, 0)))
    weighted = jnp.zeros(snapshots.shape, jnp.float32)
    for offset in range(NEIGH):
        shift_x = offset // 3 - 1
        shift_y = offset % 3 - 1
        view = padded[1 + shift_x:1 + shift_x + grid_x, 1 + shift_y:1 + shift_y + grid_y]
        chosen = jnp.sum(jnp.where((links == offset)[:, :, :, None, None], blocks, jnp.float32(0.0)), axis=2)
        weighted = weighted + jnp.einsum("abij,abjs->abis", chosen, view, precision=lax.Precision.HIGHEST)
    flattened = weighted.reshape(grid_x * grid_y * block_len, snap_cols)
    total = lax.dot_general(flattened, flattened, (((0,), (0,)), ((), ())), precision=lax.Precision.HIGHEST, preferred_element_type=jnp.float32)
    gram = total / jnp.float32(grid_x * grid_y * block_len)
    return weighted, gram
```

```python
import jax
import jax.numpy as jnp
from jax import lax
from jax.experimental import pallas as pl
from jax.experimental.pallas import tpu as pltpu
from jax.sharding import PartitionSpec as P

NEIGH = 9
BLK = 64
PLANE = ("y", "xh", "xl")
ALL = ("y", "xh", "xl", "z", "core")


def split(value):
    high = value.astype(jnp.bfloat16)
    return high, (value - high.astype(jnp.float32)).astype(jnp.bfloat16)


def weigh_kernel(
    links, side, own, x_low, x_high, y_side, corner_low, corner_high, mass, out, high, low, rhs_high, rhs_low, woven
):
    def put(place, value):
        high[place], low[place] = split(value)

    sy = side[0]
    for a in range(4):
        for b in range(4):
            put((a + 1) * 6 + b + 1, own[a * 4 + b])
    for b in range(4):
        put(b + 1, x_low[b])
        put(30 + b + 1, x_high[b])
    for column, owner in ((5, 0), (0, 1)):
        keep = (sy == owner).astype(jnp.float32)
        put(column, corner_low[...] * keep)
        put(30 + column, corner_high[...] * keep)
        for a in range(4):
            put((a + 1) * 6 + column, y_side[a] * keep)
    rhs_high[NEIGH * BLK :, :] = jnp.zeros((BLK, rhs_high.shape[1]), jnp.bfloat16)
    rhs_low[NEIGH * BLK :, :] = jnp.zeros((BLK, rhs_low.shape[1]), jnp.bfloat16)
    first = lax.broadcasted_iota(jnp.int32, (32, 128), 1) < BLK

    def block(index, carry):
        base = (index // 4) * 6 + index % 4
        evens, odds = [], []
        for k in range(NEIGH):
            code = links[index * NEIGH + k]
            source = base + (code // 3) * 6 + code % 3
            rhs_high[k * BLK : (k + 1) * BLK, :] = high[source]
            rhs_low[k * BLK : (k + 1) * BLK, :] = low[source]
        for k in range(0, NEIGH, 2):
            left = mass[index, k : k + 1, :].reshape(32, 128)
            if k + 1 < NEIGH:
                right = mass[index, k + 1 : k + 2, :].reshape(32, 128)
            else:
                right = jnp.zeros((32, 128), jnp.float32)
            evens.append(jnp.where(first, left, pltpu.roll(right, BLK, 1)))
            odds.append(jnp.where(first, pltpu.roll(left, BLK, 1), right))
        lhs = jnp.concatenate([jnp.concatenate(evens, 1), jnp.concatenate(odds, 1)], 0)
        lhs_high, lhs_low = split(lhs)
        both = jnp.dot(
            jnp.concatenate([lhs_high, lhs_low], 0), rhs_high[...], preferred_element_type=jnp.float32
        )
        total = both[:BLK] + (
            both[BLK:] + jnp.dot(lhs_high, rhs_low[...], preferred_element_type=jnp.float32)
        )
        for half in range(2):
            lanes = slice(half * 128, half * 128 + 128)
            woven[half, pl.ds(0, 32, stride=2), :] = total[:32, lanes]
            woven[half, pl.ds(1, 32, stride=2), :] = total[32:, lanes]
            out[index, :, lanes] = woven[half]
        return carry

    lax.fori_loop(0, 16, block, 0)


def weigh(snapshots, links, mass):
    sy = lax.axis_index("xl")
    edge = jnp.where(sy == 0, snapshots[:, 3], snapshots[:, 0])
    along = ("y", "xh")
    x_up = [(i, i + 1) for i in range(7)]
    x_down = [(i + 1, i) for i in range(7)]
    cross_up = [(2 * i + j, 2 * (i + 1) + 1 - j) for i in range(7) for j in range(2)]
    cross_down = [(2 * (i + 1) + j, 2 * i + 1 - j) for i in range(7) for j in range(2)]
    x_low = lax.ppermute(snapshots[3], along, x_up)
    x_high = lax.ppermute(snapshots[0], along, x_down)
    y_side = lax.ppermute(edge, "xl", [(0, 1), (1, 0)])
    corner_low = lax.ppermute(edge[3], PLANE, cross_up)
    corner_high = lax.ppermute(edge[0], PLANE, cross_down)
    cols = snapshots.shape[3]
    vmem = pl.BlockSpec(memory_space=pltpu.VMEM)
    smem = pl.BlockSpec(memory_space=pltpu.SMEM)
    out = pl.pallas_call(
        weigh_kernel,
        out_shape=jax.ShapeDtypeStruct((16, BLK, cols), jnp.float32),
        in_specs=[smem, smem] + [vmem] * 7,
        out_specs=vmem,
        scratch_shapes=[
            pltpu.VMEM((36, BLK, cols), jnp.bfloat16),
            pltpu.VMEM((36, BLK, cols), jnp.bfloat16),
            pltpu.VMEM(((NEIGH + 1) * BLK, cols), jnp.bfloat16),
            pltpu.VMEM(((NEIGH + 1) * BLK, cols), jnp.bfloat16),
            pltpu.VMEM((2, BLK, 128), jnp.float32),
        ],
        compiler_params=pltpu.CompilerParams(vmem_limit_bytes=40 * 1024 * 1024),
        cost_estimate=pl.CostEstimate(flops=10**9, bytes_accessed=6 * 10**6, transcendentals=0),
    )(
        links.reshape(-1),
        sy.reshape(1).astype(jnp.int32),
        snapshots.reshape(16, BLK, cols),
        x_low,
        x_high,
        y_side,
        corner_low,
        corner_high,
        mass.reshape(16, NEIGH, 4096),
    )
    return out


VMEM = pl.BlockSpec(memory_space=pltpu.VMEM)
SMEM = pl.BlockSpec(memory_space=pltpu.SMEM)


def dot(left, right):
    def one(a, b):
        return lax.dot_general(a, b, (((0,), (0,)), ((), ())), preferred_element_type=jnp.float32)

    return one(left[0], right[0]) + (one(left[0], right[1]) + one(left[1], right[0]))


def square_kernel(core, own, other, out):
    mine = core[0]
    parts = (split(own[...]), split(other[...]))
    sides = (mine, 1 - mine)
    for row in range(2):
        for column in range(2):
            block = dot(parts[row], parts[column])
            for i in range(2):
                for j in range(2):
                    out[4 * (2 * sides[row] + i) + 2 * sides[column] + j] = block[
                        i * 128 : i * 128 + 128, j * 128 : j * 128 + 128
                    ]


def near_kernel(core, held, last, own, other, out):
    mine = core[0]
    rights = (split(own[...]), split(other[...]))
    sides = (mine, 1 - mine)
    for index, left in enumerate((held, last)):
        left = split(left[...])
        slot = mine if index == 0 else 1 - mine
        for column in range(2):
            block = dot(left, rights[column])
            for i in range(2):
                for j in range(2):
                    out[slot, 4 * i + 2 * sides[column] + j] = block[
                        i * 128 : i * 128 + 128, j * 128 : j * 128 + 128
                    ]


def far_kernel(core, last, own, other, opposite, out):
    mine = core[0]
    rights = (split(own[...]), split(other[...]))
    sides = (mine, 1 - mine)
    left = split(last[...])
    for column in range(2):
        block = dot(left, rights[column])
        for i in range(2):
            for j in range(2):
                out[mine, 4 * i + 2 * sides[column] + j] = block[
                    i * 128 : i * 128 + 128, j * 128 : j * 128 + 128
                ]
    block = dot(left, split(opposite[...]))
    for i in range(2):
        for j in range(2):
            out[1 - mine, 4 * i + j] = block[i * 128 : i * 128 + 128, j * 128 : j * 128 + 128]
            out[1 - mine, 4 * i + 2 + j] = jnp.zeros((128, 128), jnp.float32)


def product(kernel, shape, core, *arrays):
    return pl.pallas_call(
        kernel,
        out_shape=jax.ShapeDtypeStruct(shape + (128, 128), jnp.float32),
        in_specs=[SMEM] + [VMEM] * len(arrays),
        out_specs=VMEM,
        compiler_params=pltpu.CompilerParams(vmem_limit_bytes=48 * 1024 * 1024),
        cost_estimate=pl.CostEstimate(flops=2 * 10**9, bytes_accessed=5 * 2**20, transcendentals=0),
    )(core.reshape(1).astype(jnp.int32), *arrays)


def joined(blocks):
    return jnp.concatenate([blocks[0], lax.ppermute(blocks[1], "core", SWAP)], 0)


def scatter(blocks):
    return jnp.sum(lax.all_to_all(blocks, PLANE, 0, 0, tiled=True), 0)


SWAP = [(0, 1), (1, 0)]
FIRST = (1, 3, 0, 2)


def flat(z, core, column):
    return (column % 16) * 16 + 2 * (z % 8) + core


def crossed(z, core):
    return core if z % 8 < 4 else 1 - core


def routes(turn, far):
    pairs = []
    for i in range(4):
        for j in range(4):
            low, high = 2 * (i % 2) + j % 2, 2 * (j % 2) + i % 2
            for z in range(8):
                for core in range(2):
                    here = flat(z, core, 4 * i + j)
                    row = i // 2 if core == 0 else 1 - i // 2
                    column = j // 2
                    if not far:
                        a, b = (z, z + 1) if core == 0 else (z - 1, z + 1)
                    else:
                        a, b = (z - 2, z + 1) if core == 0 else (z - 2, z + 2)
                        if core == 1:
                            if j > 1:
                                continue
                            column = crossed(z, row)
                    if low == turn:
                        pairs.append((here, flat(a, row, 2 * b + column)))
                    if (high + 2) % 4 == turn:
                        pairs.append((here, flat(b, column, 2 * a + row)))
                    if FIRST[low] == turn and core == 1 and not far:
                        pairs.append((here, flat(z, i // 2, 2 * z + j // 2)))
    return pairs


def body(snapshots, links, mass):
    y, x = lax.axis_index("y"), 2 * lax.axis_index("xh") + lax.axis_index("xl")
    z, core = lax.axis_index("z"), lax.axis_index("core")
    up = [(i, (i + 1) % 8) for i in range(8)]
    down = [(i, (i - 1) % 8) for i in range(8)]
    down_crossed = [
        (2 * i + c, 2 * ((i - 1) % 8) + crossed(i - 1, c)) for i in range(8) for c in range(2)
    ]
    weighted = weigh(snapshots, links, mass)
    held = weighted.reshape(1024, weighted.shape[2])
    next_1 = lax.ppermute(held, "z", down)
    last_1 = lax.ppermute(held, "z", up)
    held_other = lax.ppermute(held, "core", SWAP)
    square = scatter(product(square_kernel, (16,), core, held, held_other))
    next_1, last_1, square = lax.optimization_barrier((next_1, last_1, square))
    next_2 = lax.ppermute(next_1, ("z", "core"), down_crossed)
    last_2 = lax.ppermute(last_1, "z", up)
    next_other = lax.ppermute(next_1, "core", SWAP)
    near = scatter(joined(product(near_kernel, (2, 8), core, held, last_1, next_1, next_other)))
    low = 2 * (y % 2) + x % 2
    high = 2 * (x % 2) + y % 2
    next_2, last_2, near = lax.optimization_barrier((next_2, last_2, near))
    near_turned = near.T
    got = []
    for turn in range(4):
        value = jnp.where(low == turn, near, jnp.where((high + 2) % 4 == turn, near_turned, square))
        got.append(lax.ppermute(value, ALL, routes(turn, False)))
    far = scatter(
        joined(product(far_kernel, (2, 8), core, last_2, next_1, next_other, next_2))
    )
    far_turned = far.T
    for turn in range(4):
        value = jnp.where(low == turn, far, far_turned)
        got[turn] = got[turn] + lax.ppermute(value, ALL, routes(turn, True))
    column = 4 * y + x
    apart = (column // 2 - z) % 8
    over = (z + 2) % 8
    straight = (column % 2) == jnp.where(over < 4, core, 1 - core)
    mirrored = (apart > 4) | ((apart == 4) & jnp.logical_not(straight))
    part = [
        jnp.where(apart == 0, got[FIRST[k]], jnp.where(mirrored, got[(k + 2) % 4], got[k]))
        for k in range(4)
    ]
    gram = jnp.concatenate(
        [jnp.concatenate(part[:2], 1), jnp.concatenate(part[2:], 1)], 0
    ) * jnp.float32(1.0 / 16384)
    return weighted.reshape(snapshots.shape), gram


def solution(mesh):
    parts = jax.sharding.Mesh(mesh.devices.reshape(4, 2, 2, 8, 2), ALL)
    along, side, snap = ("y", "xh"), "xl", ("z", "core")
    placed = (P(along, side, None, snap), P(along, side, None), P(along, side, None, None))
    return jax.shard_map(
        body,
        mesh=parts,
        in_specs=placed,
        out_specs=(P(along, side, None, snap), P(snap, PLANE)),
        check_vma=False,
    )
```

```python
import jax
import jax.numpy as jnp
from jax import lax
from jax.experimental import pallas as pl
from jax.experimental.pallas import tpu as pltpu
from jax.sharding import PartitionSpec as P

NEIGH = 9
BLK = 64
PLANE = ("y", "xh", "xl")
ALL = ("y", "xh", "xl", "z", "core")
SWAP = [(0, 1), (1, 0)]
UP = [(k, (k + 1) % 8) for k in range(8)]
DOWN = [(k, (k - 1) % 8) for k in range(8)]
VMEM = pl.BlockSpec(memory_space=pltpu.VMEM)
SMEM = pl.BlockSpec(memory_space=pltpu.SMEM)
CORE, SIDE, ROW, COLUMN, TURN, MIRROR, KEEP = range(7)


def split(value):
    high = value.astype(jnp.bfloat16)
    return high, (value - high.astype(jnp.float32)).astype(jnp.bfloat16)


def call(kernel, shape, scratch, scalars, *arrays, after=()):
    lead = len(scalars) + len(arrays)

    def ordered(*refs):
        kernel(*refs[:lead], *refs[lead + len(after) :])

    return pl.pallas_call(
        ordered,
        out_shape=shape,
        in_specs=[SMEM] * len(scalars)
        + [VMEM] * len(arrays)
        + [pl.BlockSpec(memory_space=pl.ANY)] * len(after),
        out_specs=jax.tree.map(lambda _: VMEM, shape),
        scratch_shapes=scratch,
        compiler_params=pltpu.CompilerParams(vmem_limit_bytes=40 * 1024 * 1024),
        cost_estimate=pl.CostEstimate(flops=1, bytes_accessed=1, transcendentals=0),
    )(*scalars, *arrays, *after)


def stencil(factors, highs, lows):
    first = lax.broadcasted_iota(jnp.int32, (32, 128), 1) < BLK
    highs, lows = list(highs), list(lows)
    evens, odds = [], []
    for k in range(0, len(factors), 2):
        left = factors[k]
        if k + 1 < len(factors):
            right = factors[k + 1]
        else:
            right = jnp.zeros((32, 128), jnp.float32)
            highs.append(highs[-1])
            lows.append(lows[-1])
        evens.append(jnp.where(first, left, pltpu.roll(right, BLK, 1)))
        odds.append(jnp.where(first, pltpu.roll(left, BLK, 1), right))
    lhs = jnp.concatenate([jnp.concatenate(evens, 1), jnp.concatenate(odds, 1)], 0)
    lhs_high, lhs_low = split(lhs)
    both = jnp.dot(
        jnp.concatenate([lhs_high, lhs_low], 0),
        jnp.concatenate(highs, 0),
        preferred_element_type=jnp.float32,
    )
    return both[:BLK] + (
        both[BLK:]
        + jnp.dot(lhs_high, jnp.concatenate(lows, 0), preferred_element_type=jnp.float32)
    )


def factor(mass, a, k, b):
    return mass[a, k, b : b + 1, :].reshape(32, 128)


def halves(count, cols):
    return [pltpu.VMEM((count, BLK, cols), jnp.bfloat16)] * 2


def weave(out, at, woven, value):
    for half in range(2):
        lanes = slice(half * 128, half * 128 + 128)
        woven[half, pl.ds(0, 32, stride=2), :] = value[:32, lanes]
        woven[half, pl.ds(1, 32, stride=2), :] = value[32:, lanes]
        out[at, :, lanes] = woven[half]


def side_terms(spot, places, mass, a, high, low):
    side = spot[SIDE]
    factors = []
    for shift in range(3):
        place = places[(a * 4 + 3 - 3 * side) * NEIGH + shift * 3 + 2 - 2 * side]
        factors.append(
            jnp.where(side == 0, factor(mass, a, place, 3), factor(mass, a, place, 0))
        )
    return stencil(
        factors, [high[a + shift] for shift in range(3)], [low[a + shift] for shift in range(3)]
    )


def weigh_mid(spot, places, own, y_side, mass, mid, outer, total, high, low, y_high, y_low, woven):
    for block in range(16):
        high[block], low[block] = split(own[block])
    for a in range(4):
        y_high[1 + a], y_low[1 + a] = split(y_side[a])
    for a in range(4):
        for b in range(4):
            factors, highs, lows = [], [], []
            for code in range(NEIGH):
                row, column = a + code // 3 - 1, b + code % 3 - 1
                if 0 <= row < 4 and 0 <= column < 4:
                    factors.append(factor(mass, a, places[(a * 4 + b) * NEIGH + code], b))
                    highs.append(high[row * 4 + column])
                    lows.append(low[row * 4 + column])
            value = stencil(factors, highs, lows)
            if a in (1, 2):
                total[a * 4 - 4 + b] = value
            else:
                outer[a // 3 * 4 + b] = value
    b = 3 - 3 * spot[SIDE]
    for a in (1, 2):
        at = a * 4 - 4 + b
        total[at] = total[at] + side_terms(spot, places, mass, a, y_high, y_low)
    for block in range(8):
        weave(mid, block, woven, total[block])


def weigh_outer(
    spot, places, part, x_low, x_high, y_side, corners, mass, mid, outer, out, total, high, low, y_high, y_low, woven
):
    for b in range(4):
        high[b], low[b] = split(x_low[b])
        high[4 + b], low[4 + b] = split(x_high[b])
        y_high[1 + b], y_low[1 + b] = split(y_side[b])
    y_high[0], y_low[0] = split(corners[0])
    y_high[5], y_low[5] = split(corners[1])
    for a, code_at, halo in ((0, 0, 0), (3, 6, 4)):
        for b in range(4):
            factors, highs, lows = [], [], []
            for shift in range(3):
                column = b + shift - 1
                if 0 <= column < 4:
                    place = places[(a * 4 + b) * NEIGH + code_at + shift]
                    factors.append(factor(mass, a, place, b))
                    highs.append(high[halo + column])
                    lows.append(low[halo + column])
            total[halo + b] = part[halo + b] + stencil(factors, highs, lows)
        at = halo + 3 - 3 * spot[SIDE]
        total[at] = total[at] + side_terms(spot, places, mass, a, y_high, y_low)
    for block in range(8):
        weave(outer, block, woven, total[block])
    out[:4] = outer[:4]
    out[4:12] = mid[...]
    out[12:] = outer[4:]


def weigh(spot, snapshots, links, mass):
    side = lax.axis_index("xl")
    edge = jnp.where(side == 0, snapshots[:, 3], snapshots[:, 0])
    along = ("y", "xh")
    y_side = lax.ppermute(edge, "xl", SWAP)
    x_low = lax.ppermute(snapshots[3], along, [(i, i + 1) for i in range(7)])
    x_high = lax.ppermute(snapshots[0], along, [(i + 1, i) for i in range(7)])
    cols = snapshots.shape[3]
    codes = jnp.arange(NEIGH, dtype=jnp.int32)
    places = jnp.sum(
        jnp.where(links.reshape(16, NEIGH, 1) == codes, codes[:, None], 0), axis=1
    ).reshape(-1)
    mass = mass.transpose(0, 2, 1, 3)

    def blocks(count):
        return jax.ShapeDtypeStruct((count, BLK, cols), jnp.float32)

    total, woven = pltpu.VMEM((8, BLK, cols), jnp.float32), pltpu.VMEM((2, BLK, 128), jnp.float32)
    mid, part = call(
        weigh_mid,
        [blocks(8)] * 2,
        [total] + halves(16, cols) + halves(6, cols) + [woven],
        [spot, places],
        snapshots.reshape(16, BLK, cols),
        y_side,
        mass,
    )
    flat = mid.reshape(8 * BLK, cols)
    early = [lax.ppermute(flat, "z", UP), lax.ppermute(flat, "z", DOWN)]
    x_low, x_high, mid = lax.optimization_barrier((x_low, x_high, mid))
    corners = jnp.where(
        side == 0, jnp.stack([x_low[3], x_high[3]]), jnp.stack([x_low[0], x_high[0]])
    )
    corners = lax.ppermute(corners, "xl", SWAP)
    outer, weighted = call(
        weigh_outer,
        [blocks(8), blocks(16)],
        [total] + halves(8, cols) + halves(6, cols) + [woven],
        [spot, places],
        part,
        x_low,
        x_high,
        y_side,
        corners,
        mass,
        mid,
        after=early,
    )
    return flat, outer.reshape(8 * BLK, cols), weighted, early


def dot(left, right):
    def one(a, b):
        return lax.dot_general(a, b, (((0,), (0,)), ((), ())), preferred_element_type=jnp.float32)

    return one(left[0], right[0]) + (one(left[0], right[1]) + one(left[1], right[0]))


def whole(pair):
    parts = [split(ref[...]) for ref in pair]
    return tuple(jnp.concatenate([parts[0][k], parts[1][k]], 0) for k in range(2))


def columns(value, start, stop):
    return tuple(part[:, start:stop] for part in value)


def lay(out, at, block):
    for i in range(2):
        for j in range(2):
            out[at + 4 * i + j, :128, :] = block[i * 128 : i * 128 + 128, j * 128 : j * 128 + 128]


def near_kernel(spot, *refs):
    *arrays, out, square, relay_a, relay_b = refs
    mine = spot[CORE]
    for relay, own, other in zip((relay_a, relay_b), arrays[4:6], arrays[6:8]):
        relay[...] = jnp.where(spot[KEEP] == 1, own[...], other[...])
    held, last, own, other = [whole(arrays[k : k + 2]) for k in range(0, 8, 2)]
    for side, right in ((mine, own), (1 - mine, other)):
        lay(out, 2 * side, dot(held, right))
        lay(out, 8 + 2 * side, dot(last, right))
    first = mine == 0
    left = tuple(
        jnp.where(first, a, b) for a, b in zip(columns(own, 0, 128), columns(other, 128, 256))
    )
    right = tuple(jnp.where(first, a, b) for a, b in zip(other, own))
    cross = dot(left, right)
    square[...] = jnp.zeros(square.shape, jnp.float32)
    square[0, :128, :] = cross[:, :128]
    square[1, :128, :] = cross[:, 128:]
    diagonal = dot(own, own)
    row = lax.broadcasted_iota(jnp.int32, (128, 128), 0)
    column = lax.broadcasted_iota(jnp.int32, (128, 128), 1)
    low_end = diagonal[128:, 128:]
    square[2, :128, :] = jnp.where(row <= column, diagonal[:128, :128], low_end)
    square[2, 128:129, :] = jnp.sum(jnp.where(row == column, low_end, 0.0), 0, keepdims=True)
    square[3, :128, :] = diagonal[:128, 128:]


def far_kernel(spot, *refs):
    *arrays, square, out = refs
    mine = spot[CORE]
    last, own, other, opposite = [whole(arrays[k : k + 2]) for k in range(0, 8, 2)]
    out[:, 128:, :] = jnp.zeros((16, 8, 128), jnp.float32)
    for side, right in ((mine, own), (1 - mine, other)):
        lay(out, 2 * side, dot(last, right))
    lay(out, 8, dot(last, opposite))
    out[10:12] = square[:2]
    out[14:16] = square[2:]


def add_kernel(blocks, out):
    total = blocks[0]
    for piece in range(1, 16):
        total = total + blocks[piece]
    out[...] = total


def send_kernel(spot, far, far_beside, near, near_beside, *outs):
    y, x, core = spot[ROW], spot[COLUMN], spot[CORE]
    beside = x % 2
    even = jnp.where(beside == 0, far[...], far_beside[...])
    odd = jnp.where(beside == 0, far_beside[...], far[...])[:128]
    row = lax.broadcasted_iota(jnp.int32, (128, 128), 0)
    column = lax.broadcasted_iota(jnp.int32, (128, 128), 1)
    packed = even[:128]
    upper = jnp.where(row <= column, packed, 0.0)
    upper = upper + jnp.where(row < column, packed, 0.0).T
    lower = jnp.where(row > column, packed, 0.0)
    lower = lower + lower.T + jnp.where(row == column, even[128:129], 0.0)
    diagonal = (y == 3) & (x >= 2)
    lefts = jnp.where(diagonal, jnp.where(beside == 0, upper, odd.T), packed)
    rights = jnp.where(diagonal & (beside == 1), lower, odd)
    near_left = jnp.where(beside == 0, near[...], near_beside[...])
    near_right = jnp.where(beside == 0, near_beside[...], near[...])
    late = (y + beside + core) % 2
    for turn in range(2):
        outs[turn][:, :128] = jnp.where(late == turn, lefts, near_left)
        outs[turn][:, 128:] = jnp.where(late == turn, rights, near_right)


def place_kernel(spot, first, second, out):
    block = jnp.concatenate([first[...], second[...]], 0)
    swapped = jnp.concatenate([second[...], first[...]], 0)
    block = jnp.where(spot[TURN] == 0, block, swapped) * (1.0 / 16384)
    out[...] = jnp.where(spot[MIRROR] == 0, block, block.T)


def array(*shape):
    return jax.ShapeDtypeStruct(shape, jnp.float32)


def exchange(blocks):
    return lax.all_to_all(blocks, PLANE, 0, 0, tiled=True)


def gathered(blocks):
    total = call(add_kernel, array(*blocks.shape[1:]), [], [], blocks)
    return total, lax.ppermute(total, "xl", SWAP)


def crossed(z, core):
    return core if z % 8 < 4 else 1 - core


def routes(turn):
    pairs = []

    def flat(z, core, column):
        return (column % 16) * 16 + 2 * (z % 8) + core

    for i in range(4):
        for j in range(4):
            for z in range(8):
                for core in range(2):
                    late = turn == (i + j + core) % 2
                    mirror = j % 2 == 1
                    here = flat(z, core, 4 * i + j)
                    column = j // 2
                    if i < 2:
                        a, b = (z - 2, z + 1) if late else (z, z + 1)
                    elif not late:
                        a, b = z - 1, z + 1
                    elif j < 2:
                        a, b, column = z - 2, z + 2, crossed(z, core)
                    else:
                        row = 0 if i == 2 else core
                        column = 1 if i == 2 else core
                        if i == 3:
                            mirror = False
                        a = b = z + 1
                        pairs.append(
                            (here, flat(b, column, 2 * a + row) if mirror else flat(a, row, 2 * b + column))
                        )
                        continue
                    pairs.append(
                        (here, flat(b, column, 2 * a + core) if mirror else flat(a, core, 2 * b + column))
                    )
    return pairs


def body(snapshots, links, mass):
    y, x = lax.axis_index("y"), 2 * lax.axis_index("xh") + lax.axis_index("xl")
    z, core = lax.axis_index("z"), lax.axis_index("core")
    other = x % 2
    apart = ((4 * y + x) // 2 - z) % 8
    straight = other == jnp.where((z + 2) % 8 < 4, core, 1 - core)
    mirror = (apart > 4) | ((apart == 4) & jnp.logical_not(straight))
    mirror = mirror | ((apart == 0) & (core == 1) & (other == 0))
    turn = jnp.where(mirror, 1 - other, core)
    turn = jnp.where((apart == 1) | (apart == 2) | ((apart == 0) & (core == other)), 1 - core, turn)
    turn = jnp.where(apart > 5, other, turn)
    turn = jnp.where((apart == 0) & (core != other), core, turn)
    keep = (z + 7) % 8 < 4
    spot = [core, lax.axis_index("xl"), y, x, turn, mirror, keep]
    spot = jnp.stack([jnp.asarray(value).astype(jnp.int32) for value in spot])
    *held, weighted, early = weigh(spot, snapshots, links, mass)
    next_1 = [early[1], lax.ppermute(held[1], "z", DOWN)]
    last_1 = [early[0], lax.ppermute(held[1], "z", UP)]
    last_2 = [lax.ppermute(half, "z", UP) for half in last_1]
    next_other = [lax.ppermute(half, "core", SWAP) for half in next_1]
    near, square, *relay = call(
        near_kernel,
        [array(16, 128, 128), array(4, 136, 128)] + [array(*held[0].shape)] * 2,
        [],
        [spot],
        *held,
        *last_1,
        *next_1,
        *next_other,
    )
    next_2 = [lax.ppermute(half, "z", DOWN) for half in relay]
    near = lax.cond(links[0, 0, 0] >= 0, exchange, lambda blocks: blocks, near)
    near, near_beside = gathered(near)
    *late, near, near_beside = lax.optimization_barrier((*next_2, *last_2, near, near_beside))
    next_2, last_2 = late[:2], late[2:]
    far = call(
        far_kernel,
        array(16, 136, 128),
        [],
        [spot],
        *last_2,
        *next_1,
        *next_other,
        *next_2,
        square,
    )
    far, far_beside = gathered(exchange(far))
    sent = call(
        send_kernel, [array(128, 256)] * 2, [], [spot], far, far_beside, near, near_beside
    )
    got = [lax.ppermute(sent[k], ALL, routes(k)) for k in range(2)]
    gram = call(place_kernel, array(256, 256), [], [spot], *got)
    return weighted.reshape(snapshots.shape), gram


def solution(mesh):
    parts = jax.sharding.Mesh(mesh.devices.reshape(4, 2, 2, 8, 2), ALL)
    along, side, snap = ("y", "xh"), "xl", ("z", "core")
    placed = (P(along, side, None, snap), P(along, side, None), P(along, side, None, None))
    return jax.shard_map(
        body,
        mesh=parts,
        in_specs=placed,
        out_specs=(P(along, side, None, snap), P(snap, PLANE)),
        check_vma=False,
    )
```

```python
import jax
import jax.numpy as jnp
from jax import lax
from jax.experimental import pallas as pl
from jax.experimental.pallas import tpu as pltpu
from jax.sharding import PartitionSpec as P

NEIGH = 9
BLK = 64
PLANE = ("y", "xh", "xl")
ALL = ("y", "xh", "xl", "z", "core")
SWAP = [(0, 1), (1, 0)]
UP = [(k, (k + 1) % 8) for k in range(8)]
DOWN = [(k, (k - 1) % 8) for k in range(8)]


def turned(z):
    return (z + 3) % 8 // 4 ^ 1


DOWN_TURNED = [
    (2 * k + c, 2 * ((k - 1) % 8) + (c ^ turned(k - 1))) for k in range(8) for c in range(2)
]
VMEM = pl.BlockSpec(memory_space=pltpu.VMEM)
SMEM = pl.BlockSpec(memory_space=pltpu.SMEM)
CORE, SIDE, ROW, COLUMN, TURN, MIRROR, OWN = range(7)


def split(value):
    high = value.astype(jnp.bfloat16)
    return high, (value - high.astype(jnp.float32)).astype(jnp.bfloat16)


def call(kernel, shape, scratch, scalars, *arrays, after=()):
    lead = len(scalars) + len(arrays)

    def ordered(*refs):
        kernel(*refs[:lead], *refs[lead + len(after) :])

    return pl.pallas_call(
        ordered,
        out_shape=shape,
        in_specs=[SMEM] * len(scalars)
        + [VMEM] * len(arrays)
        + [pl.BlockSpec(memory_space=pl.ANY)] * len(after),
        out_specs=jax.tree.map(lambda _: VMEM, shape),
        scratch_shapes=scratch,
        compiler_params=pltpu.CompilerParams(vmem_limit_bytes=40 * 1024 * 1024),
        cost_estimate=pl.CostEstimate(flops=1, bytes_accessed=1, transcendentals=0),
    )(*scalars, *arrays, *after)


def stencil(factors, highs, lows):
    first = lax.broadcasted_iota(jnp.int32, (32, 128), 1) < BLK
    highs, lows = list(highs), list(lows)
    evens, odds = [], []
    for k in range(0, len(factors), 2):
        left = factors[k]
        if k + 1 < len(factors):
            right = factors[k + 1]
        else:
            right = jnp.zeros((32, 128), jnp.float32)
            highs.append(highs[-1])
            lows.append(lows[-1])
        evens.append(jnp.where(first, left, pltpu.roll(right, BLK, 1)))
        odds.append(jnp.where(first, pltpu.roll(left, BLK, 1), right))
    lhs = jnp.concatenate([jnp.concatenate(evens, 1), jnp.concatenate(odds, 1)], 0)
    lhs_high, lhs_low = split(lhs)
    both = jnp.dot(
        jnp.concatenate([lhs_high, lhs_low], 0),
        jnp.concatenate(highs, 0),
        preferred_element_type=jnp.float32,
    )
    return both[:BLK] + (
        both[BLK:]
        + jnp.dot(lhs_high, jnp.concatenate(lows, 0), preferred_element_type=jnp.float32)
    )


def factor(mass, a, k, b):
    return mass[a, k, b : b + 1, :].reshape(32, 128)


def halves(count, cols):
    return [pltpu.VMEM((count, BLK, cols), jnp.bfloat16)] * 2


def weave(out, at, woven, value):
    for half in range(2):
        lanes = slice(half * 128, half * 128 + 128)
        woven[half, pl.ds(0, 32, stride=2), :] = value[:32, lanes]
        woven[half, pl.ds(1, 32, stride=2), :] = value[32:, lanes]
        out[at, :, lanes] = woven[half]


def side_terms(spot, places, mass, a, high, low):
    side = spot[SIDE]
    factors = []
    for shift in range(3):
        place = places[(a * 4 + 3 - 3 * side) * NEIGH + shift * 3 + 2 - 2 * side]
        factors.append(
            jnp.where(side == 0, factor(mass, a, place, 3), factor(mass, a, place, 0))
        )
    return stencil(
        factors, [high[a + shift] for shift in range(3)], [low[a + shift] for shift in range(3)]
    )


def weigh_mid(spot, places, own, y_side, mass, mid, outer, total, high, low, y_high, y_low, woven):
    for block in range(16):
        high[block], low[block] = split(own[block])
    for a in range(4):
        y_high[1 + a], y_low[1 + a] = split(y_side[a])
    for a in range(4):
        for b in range(4):
            factors, highs, lows = [], [], []
            for code in range(NEIGH):
                row, column = a + code // 3 - 1, b + code % 3 - 1
                if 0 <= row < 4 and 0 <= column < 4:
                    factors.append(factor(mass, a, places[(a * 4 + b) * NEIGH + code], b))
                    highs.append(high[row * 4 + column])
                    lows.append(low[row * 4 + column])
            value = stencil(factors, highs, lows)
            if a in (1, 2):
                total[a * 4 - 4 + b] = value
            else:
                outer[a // 3 * 4 + b] = value
    b = 3 - 3 * spot[SIDE]
    for a in (1, 2):
        at = a * 4 - 4 + b
        total[at] = total[at] + side_terms(spot, places, mass, a, y_high, y_low)
    for block in range(8):
        weave(mid, block, woven, total[block])


def weigh_outer(
    spot, places, part, x_low, x_high, y_side, corners, mass, mid, outer, out, total, high, low, y_high, y_low, woven
):
    for b in range(4):
        high[b], low[b] = split(x_low[b])
        high[4 + b], low[4 + b] = split(x_high[b])
        y_high[1 + b], y_low[1 + b] = split(y_side[b])
    y_high[0], y_low[0] = split(corners[0])
    y_high[5], y_low[5] = split(corners[1])
    for a, code_at, halo in ((0, 0, 0), (3, 6, 4)):
        for b in range(4):
            factors, highs, lows = [], [], []
            for shift in range(3):
                column = b + shift - 1
                if 0 <= column < 4:
                    place = places[(a * 4 + b) * NEIGH + code_at + shift]
                    factors.append(factor(mass, a, place, b))
                    highs.append(high[halo + column])
                    lows.append(low[halo + column])
            total[halo + b] = part[halo + b] + stencil(factors, highs, lows)
        at = halo + 3 - 3 * spot[SIDE]
        total[at] = total[at] + side_terms(spot, places, mass, a, y_high, y_low)
    for block in range(8):
        weave(outer, block, woven, total[block])
    out[:4] = outer[:4]
    out[4:12] = mid[...]
    out[12:] = outer[4:]


def weigh(spot, snapshots, links, mass):
    side = lax.axis_index("xl")
    edge = jnp.where(side == 0, snapshots[:, 3], snapshots[:, 0])
    along = ("y", "xh")
    y_side = lax.ppermute(edge, "xl", SWAP)
    x_low = lax.ppermute(snapshots[3], along, [(i, i + 1) for i in range(7)])
    x_high = lax.ppermute(snapshots[0], along, [(i + 1, i) for i in range(7)])
    cols = snapshots.shape[3]
    codes = jnp.arange(NEIGH, dtype=jnp.int32)
    places = jnp.sum(
        jnp.where(links.reshape(16, NEIGH, 1) == codes, codes[:, None], 0), axis=1
    ).reshape(-1)
    mass = mass.transpose(0, 2, 1, 3)

    def blocks(count):
        return jax.ShapeDtypeStruct((count, BLK, cols), jnp.float32)

    total, woven = pltpu.VMEM((8, BLK, cols), jnp.float32), pltpu.VMEM((2, BLK, 128), jnp.float32)
    mid, part = call(
        weigh_mid,
        [blocks(8)] * 2,
        [total] + halves(16, cols) + halves(6, cols) + [woven],
        [spot, places],
        snapshots.reshape(16, BLK, cols),
        y_side,
        mass,
    )
    flat = mid.reshape(8 * BLK, cols)
    early = [lax.ppermute(flat, "z", UP), lax.ppermute(flat, ("z", "core"), DOWN_TURNED)]
    x_low, x_high, mid = lax.optimization_barrier((x_low, x_high, mid))
    corners = jnp.where(
        side == 0, jnp.stack([x_low[3], x_high[3]]), jnp.stack([x_low[0], x_high[0]])
    )
    corners = lax.ppermute(corners, "xl", SWAP)
    outer, weighted = call(
        weigh_outer,
        [blocks(8), blocks(16)],
        [total] + halves(8, cols) + halves(6, cols) + [woven],
        [spot, places],
        part,
        x_low,
        x_high,
        y_side,
        corners,
        mass,
        mid,
        after=early[:1],
    )
    return flat, outer.reshape(8 * BLK, cols), weighted, early


def dot(left, right):
    def one(a, b):
        return lax.dot_general(a, b, (((0,), (0,)), ((), ())), preferred_element_type=jnp.float32)

    return one(left[0], right[0]) + (one(left[0], right[1]) + one(left[1], right[0]))


def whole(pair):
    parts = [split(ref[...]) for ref in pair]
    return tuple(jnp.concatenate([parts[0][k], parts[1][k]], 0) for k in range(2))


def columns(value, start, stop):
    return tuple(part[:, start:stop] for part in value)


def lay(out, at, block):
    for i in range(2):
        for j in range(2):
            out[at + 4 * i + j, :128, :] = block[i * 128 : i * 128 + 128, j * 128 : j * 128 + 128]


def square_kernel(spot, *refs):
    *arrays, square = refs
    own, other = whole(arrays[:2]), whole(arrays[2:])
    first = spot[CORE] == 0
    left = tuple(
        jnp.where(first, a, b) for a, b in zip(columns(own, 0, 128), columns(other, 128, 256))
    )
    right = tuple(jnp.where(first, a, b) for a, b in zip(other, own))
    cross = dot(left, right)
    square[...] = jnp.zeros(square.shape, jnp.float32)
    square[0, :128, :] = cross[:, :128]
    square[1, :128, :] = cross[:, 128:]
    diagonal = dot(own, own)
    row = lax.broadcasted_iota(jnp.int32, (128, 128), 0)
    column = lax.broadcasted_iota(jnp.int32, (128, 128), 1)
    low_end = diagonal[128:, 128:]
    square[2, :128, :] = jnp.where(row <= column, diagonal[:128, :128], low_end)
    square[2, 128:129, :] = jnp.sum(jnp.where(row == column, low_end, 0.0), 0, keepdims=True)
    square[3, :128, :] = diagonal[:128, 128:]


def near_kernel(spot, *refs):
    *arrays, square, out = refs
    mine = spot[CORE]
    held, beside, last, own = [whole(arrays[k : k + 2]) for k in range(0, 8, 2)]
    out[:, 128:, :] = jnp.zeros((16, 8, 128), jnp.float32)
    lay(out, 2 * mine, dot(own, held))
    lay(out, 2 * (1 - mine), dot(own, beside))
    lay(out, 8, dot(last, own))
    out[10:12] = square[:2]
    out[14:16] = square[2:]


def far_kernel(spot, *refs):
    *arrays, out = refs
    mine = spot[OWN]
    last_2, own, other, opposite, last_1 = [whole(arrays[k : k + 2]) for k in range(0, 10, 2)]
    lay(out, 2 * mine, dot(last_2, own))
    lay(out, 2 * (1 - mine), dot(last_2, other))
    lay(out, 8, dot(last_2, opposite))
    lay(out, 10, dot(last_1, other))


def add_kernel(blocks, out):
    total = blocks[0]
    for piece in range(1, 16):
        total = total + blocks[piece]
    out[...] = total


def send_kernel(spot, far, far_beside, near, near_beside, *outs):
    y, x, core = spot[ROW], spot[COLUMN], spot[CORE]
    beside = x % 2
    even = jnp.where(beside == 0, near[...], near_beside[...])
    odd = jnp.where(beside == 0, near_beside[...], near[...])[:128]
    row = lax.broadcasted_iota(jnp.int32, (128, 128), 0)
    column = lax.broadcasted_iota(jnp.int32, (128, 128), 1)
    packed = even[:128]
    upper = jnp.where(row <= column, packed, 0.0)
    upper = upper + jnp.where(row < column, packed, 0.0).T
    lower = jnp.where(row > column, packed, 0.0)
    lower = lower + lower.T + jnp.where(row == column, even[128:129], 0.0)
    diagonal = (y == 3) & (x >= 2)
    lefts = jnp.where(diagonal, jnp.where(beside == 0, upper, odd.T), packed)
    rights = jnp.where(diagonal & (beside == 1), lower, odd)
    far_left = jnp.where(beside == 0, far[...], far_beside[...])
    far_right = jnp.where(beside == 0, far_beside[...], far[...])
    late = (y + beside + core) % 2
    for turn in range(2):
        outs[turn][:, :128] = jnp.where(late == turn, far_left, lefts)
        outs[turn][:, 128:] = jnp.where(late == turn, far_right, rights)


def place_kernel(spot, first, second, out):
    block = jnp.concatenate([first[...], second[...]], 0)
    swapped = jnp.concatenate([second[...], first[...]], 0)
    block = jnp.where(spot[TURN] == 0, block, swapped) * (1.0 / 16384)
    out[...] = jnp.where(spot[MIRROR] == 0, block, block.T)


def array(*shape):
    return jax.ShapeDtypeStruct(shape, jnp.float32)


def exchange(blocks):
    return lax.all_to_all(blocks, PLANE, 0, 0, tiled=True)


def gathered(blocks):
    total = call(add_kernel, array(*blocks.shape[1:]), [], [], blocks)
    return total, lax.ppermute(total, "xl", SWAP)


def crossed(z, core):
    return core if z % 8 < 4 else 1 - core


def routes(turn):
    pairs = []

    def flat(z, core, column):
        return (column % 16) * 16 + 2 * (z % 8) + core

    for i in range(4):
        for j in range(4):
            for z in range(8):
                for core in range(2):
                    late = turn == (i + j + core) % 2
                    mirror = j % 2 == 1
                    here = flat(z, core, 4 * i + j)
                    column = j // 2
                    row = core
                    if i < 2:
                        a, b = (z - 2, z + 1) if late else (z + 1, z)
                        row = core if late else core ^ turned(z)
                    elif j < 2 and late:
                        a, b, column = z - 2, z + 2, crossed(z, core)
                    elif j < 2 or late:
                        a, b, column = z - 1, z + 1, core ^ turned(z) ^ late
                    else:
                        a = b = z
                        row, column = (0, 1) if i == 2 else (core, core)
                        mirror = mirror and i == 2
                    there = flat(b, column, 2 * a + row) if mirror else flat(a, row, 2 * b + column)
                    pairs.append((here, there))
    return pairs


def body(snapshots, links, mass):
    y, x = lax.axis_index("y"), 2 * lax.axis_index("xh") + lax.axis_index("xl")
    z, core = lax.axis_index("z"), lax.axis_index("core")
    other = x % 2
    apart = ((4 * y + x) // 2 - z) % 8
    straight = other == jnp.where((z + 2) % 8 < 4, core, 1 - core)
    same = core == other
    after_same = other == core ^ turned(z + 1)
    before_same = core == other ^ turned(z + 7)
    mirror = (apart == 1) | (apart == 5) | (apart == 6)
    mirror = mirror | ((apart == 4) & jnp.logical_not(straight))
    mirror = mirror | ((apart == 0) & (core == 1) & (other == 0))
    turns = (
        jnp.where(same, core, 1 - core),
        other ^ turned(z),
        jnp.where(after_same, 1 - core, core),
        core,
        jnp.where(straight, core, 1 - other),
        1 - other,
        jnp.where(before_same, other, 1 - other),
        1 - core ^ turned(z + 7),
    )
    turn = sum(jnp.where(apart == k, value, 0) for k, value in enumerate(turns))
    spot = [core, lax.axis_index("xl"), y, x, turn, mirror, core ^ turned(z)]
    spot = jnp.stack([jnp.asarray(value).astype(jnp.int32) for value in spot])
    *held, weighted, early = weigh(spot, snapshots, links, mass)
    next_1 = [early[1], lax.ppermute(held[1], ("z", "core"), DOWN_TURNED)]
    last_1 = [early[0], lax.ppermute(held[1], "z", UP)]
    held_other = [lax.ppermute(half, "core", SWAP) for half in held]
    square = call(square_kernel, array(4, 136, 128), [], [spot], *held, *held_other)
    next_1[1], last_1[1], square = lax.optimization_barrier((next_1[1], last_1[1], square))
    last_2 = [lax.ppermute(half, "z", UP) for half in last_1]
    next_other = [lax.ppermute(half, "core", SWAP) for half in next_1]
    near = call(
        near_kernel,
        array(16, 136, 128),
        [],
        [spot],
        *held,
        *held_other,
        *last_1,
        *next_1,
        square,
    )
    next_2 = [lax.ppermute(half, "z", DOWN) for half in next_1]
    near = lax.cond(links[0, 0, 0] >= 0, exchange, lambda blocks: blocks, near)
    far = call(
        far_kernel,
        array(16, 128, 128),
        [],
        [spot],
        *last_2,
        *next_1,
        *next_other,
        *next_2,
        *last_1,
        after=(near,),
    )
    near, near_beside = gathered(near)
    far, far_beside = gathered(exchange(far))
    sent = call(
        send_kernel, [array(128, 256)] * 2, [], [spot], far, far_beside, near, near_beside
    )
    got = [lax.ppermute(sent[k], ALL, routes(k)) for k in range(2)]
    gram = call(place_kernel, array(256, 256), [], [spot], *got)
    return weighted.reshape(snapshots.shape), gram


def solution(mesh):
    parts = jax.sharding.Mesh(mesh.devices.reshape(4, 2, 2, 8, 2), ALL)
    along, side, snap = ("y", "xh"), "xl", ("z", "core")
    placed = (P(along, side, None, snap), P(along, side, None), P(along, side, None, None))
    return jax.shard_map(
        body,
        mesh=parts,
        in_specs=placed,
        out_specs=(P(along, side, None, snap), P(snap, PLANE)),
        check_vma=False,
    )
```

```python
import jax
import jax.numpy as jnp
from jax import lax
from jax.experimental import pallas as pl
from jax.experimental.pallas import tpu as pltpu
from jax.sharding import PartitionSpec as P

NEIGH = 9
BLK = 64
PLANE = ("y", "xh", "xl")
ALL = ("y", "xh", "xl", "z", "core")
SWAP = [(0, 1), (1, 0)]
UP = [(k, (k + 1) % 8) for k in range(8)]
DOWN = [(k, (k - 1) % 8) for k in range(8)]


def turned(z):
    return (z + 3) % 8 // 4 ^ 1


DOWN_TURNED = [
    (2 * k + c, 2 * ((k - 1) % 8) + (c ^ turned(k - 1))) for k in range(8) for c in range(2)
]
VMEM = pl.BlockSpec(memory_space=pltpu.VMEM)
SMEM = pl.BlockSpec(memory_space=pltpu.SMEM)
CORE, SIDE, ROW, COLUMN, OWN = range(5)


def split(value):
    high = value.astype(jnp.bfloat16)
    return high, (value - high.astype(jnp.float32)).astype(jnp.bfloat16)


def call(kernel, shape, scratch, scalars, *arrays, after=()):
    lead = len(scalars) + len(arrays)

    def ordered(*refs):
        kernel(*refs[:lead], *refs[lead + len(after) :])

    return pl.pallas_call(
        ordered,
        out_shape=shape,
        in_specs=[SMEM] * len(scalars)
        + [VMEM] * len(arrays)
        + [pl.BlockSpec(memory_space=pl.ANY)] * len(after),
        out_specs=jax.tree.map(lambda _: VMEM, shape),
        scratch_shapes=scratch,
        compiler_params=pltpu.CompilerParams(vmem_limit_bytes=40 * 1024 * 1024),
        cost_estimate=pl.CostEstimate(flops=1, bytes_accessed=1, transcendentals=0),
    )(*scalars, *arrays, *after)


def stencil(factors, highs, lows):
    first = lax.broadcasted_iota(jnp.int32, (32, 128), 1) < BLK
    highs, lows = list(highs), list(lows)
    evens, odds = [], []
    for k in range(0, len(factors), 2):
        left = factors[k]
        if k + 1 < len(factors):
            right = factors[k + 1]
        else:
            right = jnp.zeros((32, 128), jnp.float32)
            highs.append(highs[-1])
            lows.append(lows[-1])
        evens.append(jnp.where(first, left, pltpu.roll(right, BLK, 1)))
        odds.append(jnp.where(first, pltpu.roll(left, BLK, 1), right))
    lhs = jnp.concatenate([jnp.concatenate(evens, 1), jnp.concatenate(odds, 1)], 0)
    lhs_high, lhs_low = split(lhs)
    both = jnp.dot(
        jnp.concatenate([lhs_high, lhs_low], 0),
        jnp.concatenate(highs, 0),
        preferred_element_type=jnp.float32,
    )
    return both[:BLK] + (
        both[BLK:]
        + jnp.dot(lhs_high, jnp.concatenate(lows, 0), preferred_element_type=jnp.float32)
    )


def factor(mass, a, k, b):
    return mass[a, k, b : b + 1, :].reshape(32, 128)


def halves(count, cols):
    return [pltpu.VMEM((count, BLK, cols), jnp.bfloat16)] * 2


def weave(out, at, woven, value):
    for half in range(2):
        lanes = slice(half * 128, half * 128 + 128)
        woven[half, pl.ds(0, 32, stride=2), :] = value[:32, lanes]
        woven[half, pl.ds(1, 32, stride=2), :] = value[32:, lanes]
        out[at, :, lanes] = woven[half]


def side_terms(spot, places, mass, a, high, low):
    side = spot[SIDE]
    factors = []
    for shift in range(3):
        place = places[(a * 4 + 3 - 3 * side) * NEIGH + shift * 3 + 2 - 2 * side]
        factors.append(
            jnp.where(side == 0, factor(mass, a, place, 3), factor(mass, a, place, 0))
        )
    return stencil(
        factors, [high[a + shift] for shift in range(3)], [low[a + shift] for shift in range(3)]
    )


def weigh_mid(spot, places, own, y_side, mass, mid, outer, total, high, low, y_high, y_low, woven):
    for block in range(16):
        high[block], low[block] = split(own[block])
    for a in range(4):
        y_high[1 + a], y_low[1 + a] = split(y_side[a])
    for a in range(4):
        for b in range(4):
            factors, highs, lows = [], [], []
            for code in range(NEIGH):
                row, column = a + code // 3 - 1, b + code % 3 - 1
                if 0 <= row < 4 and 0 <= column < 4:
                    factors.append(factor(mass, a, places[(a * 4 + b) * NEIGH + code], b))
                    highs.append(high[row * 4 + column])
                    lows.append(low[row * 4 + column])
            value = stencil(factors, highs, lows)
            if a in (1, 2):
                total[a * 4 - 4 + b] = value
            else:
                outer[a // 3 * 4 + b] = value
    b = 3 - 3 * spot[SIDE]
    for a in (1, 2):
        at = a * 4 - 4 + b
        total[at] = total[at] + side_terms(spot, places, mass, a, y_high, y_low)
    for block in range(8):
        weave(mid, block, woven, total[block])


def weigh_outer(
    spot, places, part, x_low, x_high, y_side, corners, mass, mid, outer, out, total, high, low, y_high, y_low, woven
):
    for b in range(4):
        high[b], low[b] = split(x_low[b])
        high[4 + b], low[4 + b] = split(x_high[b])
        y_high[1 + b], y_low[1 + b] = split(y_side[b])
    y_high[0], y_low[0] = split(corners[0])
    y_high[5], y_low[5] = split(corners[1])
    for a, code_at, halo in ((0, 0, 0), (3, 6, 4)):
        for b in range(4):
            factors, highs, lows = [], [], []
            for shift in range(3):
                column = b + shift - 1
                if 0 <= column < 4:
                    place = places[(a * 4 + b) * NEIGH + code_at + shift]
                    factors.append(factor(mass, a, place, b))
                    highs.append(high[halo + column])
                    lows.append(low[halo + column])
            total[halo + b] = part[halo + b] + stencil(factors, highs, lows)
        at = halo + 3 - 3 * spot[SIDE]
        total[at] = total[at] + side_terms(spot, places, mass, a, y_high, y_low)
    for block in range(8):
        weave(outer, block, woven, total[block])
    out[:4] = outer[:4]
    out[4:12] = mid[...]
    out[12:] = outer[4:]


def weigh(spot, snapshots, links, mass):
    side = lax.axis_index("xl")
    edge = jnp.where(side == 0, snapshots[:, 3], snapshots[:, 0])
    along = ("y", "xh")
    y_side = lax.ppermute(edge, "xl", SWAP)
    x_low = lax.ppermute(snapshots[3], along, [(i, i + 1) for i in range(7)])
    x_high = lax.ppermute(snapshots[0], along, [(i + 1, i) for i in range(7)])
    cols = snapshots.shape[3]
    codes = jnp.arange(NEIGH, dtype=jnp.int32)
    places = jnp.sum(
        jnp.where(links.reshape(16, NEIGH, 1) == codes, codes[:, None], 0), axis=1
    ).reshape(-1)
    mass = mass.transpose(0, 2, 1, 3)

    def blocks(count):
        return jax.ShapeDtypeStruct((count, BLK, cols), jnp.float32)

    total, woven = pltpu.VMEM((8, BLK, cols), jnp.float32), pltpu.VMEM((2, BLK, 128), jnp.float32)
    mid, part = call(
        weigh_mid,
        [blocks(8)] * 2,
        [total] + halves(16, cols) + halves(6, cols) + [woven],
        [spot, places],
        snapshots.reshape(16, BLK, cols),
        y_side,
        mass,
    )
    flat = mid.reshape(8 * BLK, cols)
    early = [lax.ppermute(flat, "z", UP), lax.ppermute(flat, ("z", "core"), DOWN_TURNED)]
    x_low, x_high, mid = lax.optimization_barrier((x_low, x_high, mid))
    corners = jnp.where(
        side == 0, jnp.stack([x_low[3], x_high[3]]), jnp.stack([x_low[0], x_high[0]])
    )
    corners = lax.ppermute(corners, "xl", SWAP)
    outer, weighted = call(
        weigh_outer,
        [blocks(8), blocks(16)],
        [total] + halves(8, cols) + halves(6, cols) + [woven],
        [spot, places],
        part,
        x_low,
        x_high,
        y_side,
        corners,
        mass,
        mid,
    )
    outer, *early = lax.optimization_barrier((outer, *early))
    return flat, outer.reshape(8 * BLK, cols), weighted, early


def dot(left, right):
    def one(a, b):
        return lax.dot_general(a, b, (((0,), (0,)), ((), ())), preferred_element_type=jnp.float32)

    return one(left[0], right[0]) + (one(left[0], right[1]) + one(left[1], right[0]))


def whole(pair):
    parts = [split(ref[...]) for ref in pair]
    return tuple(jnp.concatenate([parts[0][k], parts[1][k]], 0) for k in range(2))


def columns(value, start, stop):
    return tuple(part[:, start:stop] for part in value)


def lay(out, at, block):
    for i in range(2):
        for j in range(2):
            out[at + 4 * i + j, :128, :] = block[i * 128 : i * 128 + 128, j * 128 : j * 128 + 128]


def square_kernel(spot, *refs):
    *arrays, square = refs
    own, other = whole(arrays[:2]), whole(arrays[2:])
    first = spot[CORE] == 0
    left = tuple(
        jnp.where(first, a, b) for a, b in zip(columns(own, 0, 128), columns(other, 128, 256))
    )
    right = tuple(jnp.where(first, a, b) for a, b in zip(other, own))
    cross = dot(left, right)
    square[...] = jnp.zeros(square.shape, jnp.float32)
    square[0, :128, :] = cross[:, :128]
    square[1, :128, :] = cross[:, 128:]
    diagonal = dot(own, own)
    row = lax.broadcasted_iota(jnp.int32, (128, 128), 0)
    column = lax.broadcasted_iota(jnp.int32, (128, 128), 1)
    low_end = diagonal[128:, 128:]
    square[2, :128, :] = jnp.where(row <= column, diagonal[:128, :128], low_end)
    square[2, 128:129, :] = jnp.sum(jnp.where(row == column, low_end, 0.0), 0, keepdims=True)
    square[3, :128, :] = diagonal[:128, 128:]


def near_kernel(spot, *refs):
    *arrays, square, out = refs
    mine = spot[CORE]
    held, beside, last, own = [whole(arrays[k : k + 2]) for k in range(0, 8, 2)]
    out[:, 128:, :] = jnp.zeros((16, 8, 128), jnp.float32)
    lay(out, 2 * mine, dot(own, held))
    lay(out, 2 * (1 - mine), dot(own, beside))
    lay(out, 8, dot(last, own))
    out[10:12] = square[:2]
    out[14:16] = square[2:]


def far_kernel(spot, *refs):
    *arrays, out = refs
    mine = spot[OWN]
    last_2, own, other, opposite, last_1 = [whole(arrays[k : k + 2]) for k in range(0, 10, 2)]
    lay(out, 2 * mine, dot(last_2, own))
    lay(out, 2 * (1 - mine), dot(last_2, other))
    lay(out, 8, dot(last_2, opposite))
    lay(out, 10, dot(last_1, other))


def add_kernel(blocks, out):
    total = blocks[0]
    for piece in range(1, 16):
        total = total + blocks[piece]
    out[...] = total


def send_kernel(spot, far, far_beside, near, near_beside, *outs):
    y, x, core = spot[ROW], spot[COLUMN], spot[CORE]
    beside = x % 2
    even = jnp.where(beside == 0, near[...], near_beside[...])
    odd = jnp.where(beside == 0, near_beside[...], near[...])[:128]
    row = lax.broadcasted_iota(jnp.int32, (128, 128), 0)
    column = lax.broadcasted_iota(jnp.int32, (128, 128), 1)
    packed = even[:128]
    upper = jnp.where(row <= column, packed, 0.0)
    upper = upper + jnp.where(row < column, packed, 0.0).T
    lower = jnp.where(row > column, packed, 0.0)
    lower = lower + lower.T + jnp.where(row == column, even[128:129], 0.0)
    diagonal = (y == 3) & (x >= 2)
    lefts = jnp.where(diagonal, jnp.where(beside == 0, upper, odd.T), packed)
    rights = jnp.where(diagonal & (beside == 1), lower, odd)
    far_left = jnp.where(beside == 0, far[...], far_beside[...])
    far_right = jnp.where(beside == 0, far_beside[...], far[...])
    late = (y + beside + core) % 2
    turned = (beside == 1) & jnp.logical_not(diagonal)
    lefts, rights = jnp.where(turned, lefts.T, lefts), jnp.where(turned, rights.T, rights)
    turned = beside == 1
    far_left = jnp.where(turned, far_left.T, far_left)
    far_right = jnp.where(turned, far_right.T, far_right)
    for turn in range(2):
        outs[turn][:, :128] = jnp.where(late == turn, far_left, lefts)
        outs[turn][:, 128:] = jnp.where(late == turn, far_right, rights)


def array(*shape):
    return jax.ShapeDtypeStruct(shape, jnp.float32)


def gathered(blocks):
    blocks = lax.all_to_all(blocks, PLANE, 0, 0, tiled=True)
    return call(add_kernel, array(*blocks.shape[1:]), [], [], blocks)


def crossed(z, core):
    return core if z % 8 < 4 else 1 - core


def routes(turn):
    pairs = []

    def flat(z, core, column):
        return (column % 16) * 16 + 2 * (z % 8) + core

    for i in range(4):
        for j in range(4):
            for z in range(8):
                for core in range(2):
                    late = turn == (i + j + core) % 2
                    mirror = j % 2 == 1
                    here = flat(z, core, 4 * i + j)
                    column = j // 2
                    row = core
                    if i < 2:
                        a, b = (z - 2, z + 1) if late else (z + 1, z)
                        row = core if late else core ^ turned(z)
                    elif j < 2 and late:
                        a, b, column = z - 2, z + 2, crossed(z, core)
                    elif j < 2 or late:
                        a, b, column = z - 1, z + 1, core ^ turned(z) ^ late
                    else:
                        a = b = z
                        row, column = (0, 1) if i == 2 else (core, core)
                        mirror = mirror and i == 2
                    there = flat(b, column, 2 * a + row) if mirror else flat(a, row, 2 * b + column)
                    pairs.append((here, there))
    return pairs


def body(snapshots, links, mass):
    y, x = lax.axis_index("y"), 2 * lax.axis_index("xh") + lax.axis_index("xl")
    z, core = lax.axis_index("z"), lax.axis_index("core")
    other = x % 2
    apart = ((4 * y + x) // 2 - z) % 8
    straight = other == jnp.where((z + 2) % 8 < 4, core, 1 - core)
    same = core == other
    after_same = other == core ^ turned(z + 1)
    before_same = core == other ^ turned(z + 7)
    mirror = (apart == 1) | (apart == 5) | (apart == 6)
    mirror = mirror | ((apart == 4) & jnp.logical_not(straight))
    mirror = mirror | ((apart == 0) & (core == 1) & (other == 0))
    turns = (
        jnp.where(same, core, 1 - core),
        other ^ turned(z),
        jnp.where(after_same, 1 - core, core),
        core,
        jnp.where(straight, core, 1 - other),
        1 - other,
        jnp.where(before_same, other, 1 - other),
        1 - core ^ turned(z + 7),
    )
    turn = sum(jnp.where(apart == k, value, 0) for k, value in enumerate(turns))
    spot = [core, lax.axis_index("xl"), y, x, core ^ turned(z)]
    spot = jnp.stack([jnp.asarray(value).astype(jnp.int32) for value in spot])
    *held, weighted, early = weigh(spot, snapshots, links, mass)
    next_1 = [early[1], lax.ppermute(held[1], ("z", "core"), DOWN_TURNED)]
    last_1 = [early[0], lax.ppermute(held[1], "z", UP)]
    held_other = [lax.ppermute(half, "core", SWAP) for half in held]
    square = call(square_kernel, array(4, 136, 128), [], [spot], *held, *held_other)
    sure = links[0, 0, 0] >= 0
    next_1[1], last_1[1], square, sure = lax.optimization_barrier(
        (next_1[1], last_1[1], square, sure)
    )
    near = call(
        near_kernel,
        array(16, 136, 128),
        [],
        [spot],
        *held,
        *held_other,
        *last_1,
        *next_1,
        square,
    )
    next_1[1], last_1[1], near = lax.optimization_barrier((next_1[1], last_1[1], near))
    last_2 = [lax.ppermute(half, "z", UP) for half in last_1]
    next_2 = [lax.ppermute(half, "z", DOWN) for half in next_1]
    next_other = [lax.ppermute(half, "core", SWAP) for half in next_1]
    near = lax.cond(sure, gathered, lambda blocks: blocks[0], near)
    far = call(
        far_kernel,
        array(16, 128, 128),
        [],
        [spot],
        *last_2,
        *next_1,
        *next_other,
        *next_2,
        *last_1,
        after=(near,),
    )
    near_beside = lax.ppermute(near, "xl", SWAP)
    far = gathered(far)
    far_beside = lax.ppermute(far, "xl", SWAP)
    sent = call(
        send_kernel, [array(128, 256)] * 2, [], [spot], far, far_beside, near, near_beside
    )
    got = [lax.ppermute(sent[k], ALL, routes(k)) for k in range(2)]
    first = [jnp.where(turn == 0, got[0][:, k : k + 128], got[1][:, k : k + 128]) for k in (0, 128)]
    second = [jnp.where(turn == 0, got[1][:, k : k + 128], got[0][:, k : k + 128]) for k in (0, 128)]
    upper = jnp.concatenate([first[0], jnp.where(mirror, second[0], first[1])], 1)
    lower = jnp.concatenate([jnp.where(mirror, first[1], second[0]), second[1]], 1)
    gram = jnp.concatenate([upper, lower], 0) * jnp.float32(1.0 / 16384)
    return weighted.reshape(snapshots.shape), gram


def solution(mesh):
    parts = jax.sharding.Mesh(mesh.devices.reshape(4, 2, 2, 8, 2), ALL)
    along, side, snap = ("y", "xh"), "xl", ("z", "core")
    placed = (P(along, side, None, snap), P(along, side, None), P(along, side, None, None))
    return jax.shard_map(
        body,
        mesh=parts,
        in_specs=placed,
        out_specs=(P(along, side, None, snap), P(snap, PLANE)),
        check_vma=False,
    )
```

```python
import jax
import jax.numpy as jnp
from jax import lax
from jax.experimental import pallas as pl
from jax.experimental.pallas import tpu as pltpu
from jax.sharding import PartitionSpec as P

NEIGH = 9
BLK = 64
PLANE = ("y", "xh", "xl")
ALL = ("y", "xh", "xl", "z", "core")
SWAP = [(0, 1), (1, 0)]
UP = [(k, (k + 1) % 8) for k in range(8)]
DOWN = [(k, (k - 1) % 8) for k in range(8)]


def turned(z):
    return (z + 3) % 8 // 4 ^ 1


DOWN_TURNED = [
    (2 * k + c, 2 * ((k - 1) % 8) + (c ^ turned(k - 1))) for k in range(8) for c in range(2)
]
VMEM = pl.BlockSpec(memory_space=pltpu.VMEM)
SMEM = pl.BlockSpec(memory_space=pltpu.SMEM)
CORE, SIDE, ROW, COLUMN, OWN = range(5)


def split(value):
    high = value.astype(jnp.bfloat16)
    return high, (value - high.astype(jnp.float32)).astype(jnp.bfloat16)


def call(kernel, shape, scratch, scalars, *arrays, after=()):
    lead = len(scalars) + len(arrays)

    def ordered(*refs):
        kernel(*refs[:lead], *refs[lead + len(after) :])

    return pl.pallas_call(
        ordered,
        out_shape=shape,
        in_specs=[SMEM] * len(scalars)
        + [VMEM] * len(arrays)
        + [pl.BlockSpec(memory_space=pl.ANY)] * len(after),
        out_specs=jax.tree.map(lambda _: VMEM, shape),
        scratch_shapes=scratch,
        compiler_params=pltpu.CompilerParams(vmem_limit_bytes=40 * 1024 * 1024),
        cost_estimate=pl.CostEstimate(flops=1, bytes_accessed=1, transcendentals=0),
    )(*scalars, *arrays, *after)


def stencil(factors, highs, lows):
    first = lax.broadcasted_iota(jnp.int32, (32, 128), 1) < BLK
    highs, lows = list(highs), list(lows)
    evens, odds = [], []
    for k in range(0, len(factors), 2):
        left = factors[k]
        if k + 1 < len(factors):
            right = factors[k + 1]
        else:
            right = jnp.zeros((32, 128), jnp.float32)
            highs.append(highs[-1])
            lows.append(lows[-1])
        evens.append(jnp.where(first, left, pltpu.roll(right, BLK, 1)))
        odds.append(jnp.where(first, pltpu.roll(left, BLK, 1), right))
    lhs = jnp.concatenate([jnp.concatenate(evens, 1), jnp.concatenate(odds, 1)], 0)
    lhs_high, lhs_low = split(lhs)
    both = jnp.dot(
        jnp.concatenate([lhs_high, lhs_low], 0),
        jnp.concatenate(highs, 0),
        preferred_element_type=jnp.float32,
    )
    return both[:BLK] + (
        both[BLK:]
        + jnp.dot(lhs_high, jnp.concatenate(lows, 0), preferred_element_type=jnp.float32)
    )


def factor(mass, a, k, b):
    return mass[a, k, b : b + 1, :].reshape(32, 128)


def halves(count, cols):
    return [pltpu.VMEM((count, BLK, cols), jnp.bfloat16)] * 2


def weave(out, at, woven, value):
    for half in range(2):
        lanes = slice(half * 128, half * 128 + 128)
        woven[half, pl.ds(0, 32, stride=2), :] = value[:32, lanes]
        woven[half, pl.ds(1, 32, stride=2), :] = value[32:, lanes]
        out[at, :, lanes] = woven[half]


def side_terms(spot, places, mass, a, high, low):
    side = spot[SIDE]
    factors = []
    for shift in range(3):
        place = places[(a * 4 + 3 - 3 * side) * NEIGH + shift * 3 + 2 - 2 * side]
        factors.append(
            jnp.where(side == 0, factor(mass, a, place, 3), factor(mass, a, place, 0))
        )
    return stencil(
        factors, [high[a + shift] for shift in range(3)], [low[a + shift] for shift in range(3)]
    )


def weigh_mid(spot, places, own, y_side, mass, mid, outer, total, high, low, y_high, y_low, woven):
    for block in range(16):
        high[block], low[block] = split(own[block])
    for a in range(4):
        y_high[1 + a], y_low[1 + a] = split(y_side[a])
    for a in range(4):
        for b in range(4):
            factors, highs, lows = [], [], []
            for code in range(NEIGH):
                row, column = a + code // 3 - 1, b + code % 3 - 1
                if 0 <= row < 4 and 0 <= column < 4:
                    factors.append(factor(mass, a, places[(a * 4 + b) * NEIGH + code], b))
                    highs.append(high[row * 4 + column])
                    lows.append(low[row * 4 + column])
            value = stencil(factors, highs, lows)
            if a in (1, 2):
                total[a * 4 - 4 + b] = value
            else:
                outer[a // 3 * 4 + b] = value
    b = 3 - 3 * spot[SIDE]
    for a in (1, 2):
        at = a * 4 - 4 + b
        total[at] = total[at] + side_terms(spot, places, mass, a, y_high, y_low)
    for block in range(8):
        weave(mid, block, woven, total[block])


def weigh_outer(
    spot, places, part, x_low, x_high, y_side, corners, mass, mid, outer, out, total, high, low, y_high, y_low, woven
):
    for b in range(4):
        high[b], low[b] = split(x_low[b])
        high[4 + b], low[4 + b] = split(x_high[b])
        y_high[1 + b], y_low[1 + b] = split(y_side[b])
    y_high[0], y_low[0] = split(corners[0])
    y_high[5], y_low[5] = split(corners[1])
    for a, code_at, halo in ((0, 0, 0), (3, 6, 4)):
        for b in range(4):
            factors, highs, lows = [], [], []
            for shift in range(3):
                column = b + shift - 1
                if 0 <= column < 4:
                    place = places[(a * 4 + b) * NEIGH + code_at + shift]
                    factors.append(factor(mass, a, place, b))
                    highs.append(high[halo + column])
                    lows.append(low[halo + column])
            total[halo + b] = part[halo + b] + stencil(factors, highs, lows)
        at = halo + 3 - 3 * spot[SIDE]
        total[at] = total[at] + side_terms(spot, places, mass, a, y_high, y_low)
    for block in range(8):
        weave(outer, block, woven, total[block])
    out[:4] = outer[:4]
    out[4:12] = mid[...]
    out[12:] = outer[4:]


def weigh(spot, snapshots, links, mass):
    side = lax.axis_index("xl")
    edge = jnp.where(side == 0, snapshots[:, 3], snapshots[:, 0])
    along = ("y", "xh")
    y_side = lax.ppermute(edge, "xl", SWAP)
    x_low = lax.ppermute(snapshots[3], along, [(i, i + 1) for i in range(7)])
    x_high = lax.ppermute(snapshots[0], along, [(i + 1, i) for i in range(7)])
    cols = snapshots.shape[3]
    codes = jnp.arange(NEIGH, dtype=jnp.int32)
    places = jnp.sum(
        jnp.where(links.reshape(16, NEIGH, 1) == codes, codes[:, None], 0), axis=1
    ).reshape(-1)
    mass = mass.transpose(0, 2, 1, 3)

    def blocks(count):
        return jax.ShapeDtypeStruct((count, BLK, cols), jnp.float32)

    total, woven = pltpu.VMEM((8, BLK, cols), jnp.float32), pltpu.VMEM((2, BLK, 128), jnp.float32)
    mid, part = call(
        weigh_mid,
        [blocks(8)] * 2,
        [total] + halves(16, cols) + halves(6, cols) + [woven],
        [spot, places],
        snapshots.reshape(16, BLK, cols),
        y_side,
        mass,
    )
    flat = mid.reshape(8 * BLK, cols)
    early = [lax.ppermute(flat, "z", UP), lax.ppermute(flat, ("z", "core"), DOWN_TURNED)]
    x_low, x_high, mid = lax.optimization_barrier((x_low, x_high, mid))
    corners = jnp.where(
        side == 0, jnp.stack([x_low[3], x_high[3]]), jnp.stack([x_low[0], x_high[0]])
    )
    corners = lax.ppermute(corners, "xl", SWAP)
    outer, weighted = call(
        weigh_outer,
        [blocks(8), blocks(16)],
        [total] + halves(8, cols) + halves(6, cols) + [woven],
        [spot, places],
        part,
        x_low,
        x_high,
        y_side,
        corners,
        mass,
        mid,
    )
    outer, *early = lax.optimization_barrier((outer, *early))
    return flat, outer.reshape(8 * BLK, cols), weighted, early


def dot(left, right):
    def one(a, b):
        return lax.dot_general(a, b, (((0,), (0,)), ((), ())), preferred_element_type=jnp.float32)

    return one(left[0], right[0]) + (one(left[0], right[1]) + one(left[1], right[0]))


def whole(pair):
    parts = [split(ref[...]) for ref in pair]
    return tuple(jnp.concatenate([parts[0][k], parts[1][k]], 0) for k in range(2))


def columns(value, start, stop):
    return tuple(part[:, start:stop] for part in value)


def lay(out, at, block):
    for i in range(2):
        for j in range(2):
            out[at + 4 * i + j, :128, :] = block[i * 128 : i * 128 + 128, j * 128 : j * 128 + 128]


def square_kernel(spot, *refs):
    *arrays, square = refs
    own, other = whole(arrays[:2]), whole(arrays[2:])
    first = spot[CORE] == 0
    left = tuple(
        jnp.where(first, a, b) for a, b in zip(columns(own, 0, 128), columns(other, 128, 256))
    )
    right = tuple(jnp.where(first, a, b) for a, b in zip(other, own))
    cross = dot(left, right)
    square[...] = jnp.zeros(square.shape, jnp.float32)
    square[0, :128, :] = cross[:, :128]
    square[1, :128, :] = cross[:, 128:]
    diagonal = dot(own, own)
    row = lax.broadcasted_iota(jnp.int32, (128, 128), 0)
    column = lax.broadcasted_iota(jnp.int32, (128, 128), 1)
    low_end = diagonal[128:, 128:]
    square[2, :128, :] = jnp.where(row <= column, diagonal[:128, :128], low_end)
    square[2, 128:129, :] = jnp.sum(jnp.where(row == column, low_end, 0.0), 0, keepdims=True)
    square[3, :128, :] = diagonal[:128, 128:]


def near_kernel(spot, *refs):
    *arrays, square, out = refs
    mine = spot[CORE]
    held, beside, last, own = [whole(arrays[k : k + 2]) for k in range(0, 8, 2)]
    out[:, 128:, :] = jnp.zeros((16, 8, 128), jnp.float32)
    lay(out, 2 * mine, dot(own, held))
    lay(out, 2 * (1 - mine), dot(own, beside))
    lay(out, 8, dot(last, own))
    out[10:12] = square[:2]
    out[14:16] = square[2:]


def far_kernel(spot, *refs):
    *arrays, out = refs
    mine = spot[OWN]
    last_2, own, other, opposite, last_1 = [whole(arrays[k : k + 2]) for k in range(0, 10, 2)]
    lay(out, 2 * mine, dot(last_2, own))
    lay(out, 2 * (1 - mine), dot(last_2, other))
    lay(out, 8, dot(last_2, opposite))
    lay(out, 10, dot(last_1, other))


def add_kernel(blocks, out):
    total = blocks[0]
    for piece in range(1, 16):
        total = total + blocks[piece]
    out[...] = total


def send_kernel(spot, far, far_beside, near, near_beside, *outs):
    y, x, core = spot[ROW], spot[COLUMN], spot[CORE]
    beside = x % 2
    even = jnp.where(beside == 0, near[...], near_beside[...])
    odd = jnp.where(beside == 0, near_beside[...], near[...])[:128]
    row = lax.broadcasted_iota(jnp.int32, (128, 128), 0)
    column = lax.broadcasted_iota(jnp.int32, (128, 128), 1)
    packed = even[:128]
    upper = jnp.where(row <= column, packed, 0.0)
    upper = upper + jnp.where(row < column, packed, 0.0).T
    lower = jnp.where(row > column, packed, 0.0)
    lower = lower + lower.T + jnp.where(row == column, even[128:129], 0.0)
    diagonal = (y == 3) & (x >= 2)
    lefts = jnp.where(diagonal, jnp.where(beside == 0, upper, odd.T), packed)
    rights = jnp.where(diagonal & (beside == 1), lower, odd)
    far_left = jnp.where(beside == 0, far[...], far_beside[...])
    far_right = jnp.where(beside == 0, far_beside[...], far[...])
    late = (y + beside + core) % 2
    turned = (beside == 1) & jnp.logical_not(diagonal)
    lefts, rights = jnp.where(turned, lefts.T, lefts), jnp.where(turned, rights.T, rights)
    turned = beside == 1
    far_left = jnp.where(turned, far_left.T, far_left)
    far_right = jnp.where(turned, far_right.T, far_right)
    for turn in range(2):
        outs[turn][:, :128] = jnp.where(late == turn, far_left, lefts)
        outs[turn][:, 128:] = jnp.where(late == turn, far_right, rights)


def array(*shape):
    return jax.ShapeDtypeStruct(shape, jnp.float32)


def gathered(blocks):
    blocks = lax.all_to_all(blocks, PLANE, 0, 0, tiled=True)
    return call(add_kernel, array(*blocks.shape[1:]), [], [], blocks)


def crossed(z, core):
    return core if z % 8 < 4 else 1 - core


def routes(turn):
    pairs = []

    def flat(z, core, column):
        return (column % 16) * 16 + 2 * (z % 8) + core

    for i in range(4):
        for j in range(4):
            for z in range(8):
                for core in range(2):
                    late = turn == (i + j + core) % 2
                    mirror = j % 2 == 1
                    here = flat(z, core, 4 * i + j)
                    column = j // 2
                    row = core
                    if i < 2:
                        a, b = (z - 2, z + 1) if late else (z + 1, z)
                        row = core if late else core ^ turned(z)
                    elif j < 2 and late:
                        a, b, column = z - 2, z + 2, crossed(z, core)
                    elif j < 2 or late:
                        a, b, column = z - 1, z + 1, core ^ turned(z) ^ late
                    else:
                        a = b = z
                        row, column = (0, 1) if i == 2 else (core, core)
                        mirror = mirror and i == 2
                    there = flat(b, column, 2 * a + row) if mirror else flat(a, row, 2 * b + column)
                    pairs.append((here, there))
    return pairs


def body(snapshots, links, mass):
    y, x = lax.axis_index("y"), 2 * lax.axis_index("xh") + lax.axis_index("xl")
    z, core = lax.axis_index("z"), lax.axis_index("core")
    other = x % 2
    apart = ((4 * y + x) // 2 - z) % 8
    straight = other == jnp.where((z + 2) % 8 < 4, core, 1 - core)
    same = core == other
    after_same = other == core ^ turned(z + 1)
    before_same = core == other ^ turned(z + 7)
    mirror = (apart == 1) | (apart == 5) | (apart == 6)
    mirror = mirror | ((apart == 4) & jnp.logical_not(straight))
    mirror = mirror | ((apart == 0) & (core == 1) & (other == 0))
    turns = (
        jnp.where(same, core, 1 - core),
        other ^ turned(z),
        jnp.where(after_same, 1 - core, core),
        core,
        jnp.where(straight, core, 1 - other),
        1 - other,
        jnp.where(before_same, other, 1 - other),
        1 - core ^ turned(z + 7),
    )
    turn = sum(jnp.where(apart == k, value, 0) for k, value in enumerate(turns))
    spot = [core, lax.axis_index("xl"), y, x, core ^ turned(z)]
    spot = jnp.stack([jnp.asarray(value).astype(jnp.int32) for value in spot])
    *held, weighted, early = weigh(spot, snapshots, links, mass)
    next_1 = [early[1], lax.ppermute(held[1], ("z", "core"), DOWN_TURNED)]
    last_1 = [early[0], lax.ppermute(held[1], "z", UP)]
    held_other = [lax.ppermute(half, "core", SWAP) for half in held]
    square = call(square_kernel, array(4, 136, 128), [], [spot], *held, *held_other)
    sure = links[0, 0, 0] >= 0
    next_1[1], square, sure = lax.optimization_barrier((next_1[1], square, sure))
    next_other = [lax.ppermute(half, "core", SWAP) for half in next_1]
    next_1[1], last_1[1], square, next_other[1] = lax.optimization_barrier(
        (next_1[1], last_1[1], square, next_other[1])
    )
    near = call(
        near_kernel,
        array(16, 136, 128),
        [],
        [spot],
        *held,
        *held_other,
        *last_1,
        *next_1,
        square,
    )
    next_1[1], last_1[1], near = lax.optimization_barrier((next_1[1], last_1[1], near))
    last_2 = [lax.ppermute(half, "z", UP) for half in last_1]
    next_2 = [lax.ppermute(half, "z", DOWN) for half in next_1]
    near = lax.cond(sure, gathered, lambda blocks: blocks[0], near)
    far = call(
        far_kernel,
        array(16, 128, 128),
        [],
        [spot],
        *last_2,
        *next_1,
        *next_other,
        *next_2,
        *last_1,
        after=(near,),
    )
    near_beside = lax.ppermute(near, "xl", SWAP)
    far = gathered(far)
    far_beside = lax.ppermute(far, "xl", SWAP)
    sent = call(
        send_kernel, [array(128, 256)] * 2, [], [spot], far, far_beside, near, near_beside
    )
    got = [lax.ppermute(sent[k], ALL, routes(k)) for k in range(2)]
    first = [jnp.where(turn == 0, got[0][:, k : k + 128], got[1][:, k : k + 128]) for k in (0, 128)]
    second = [jnp.where(turn == 0, got[1][:, k : k + 128], got[0][:, k : k + 128]) for k in (0, 128)]
    upper = jnp.concatenate([first[0], jnp.where(mirror, second[0], first[1])], 1)
    lower = jnp.concatenate([jnp.where(mirror, first[1], second[0]), second[1]], 1)
    gram = jnp.concatenate([upper, lower], 0) * jnp.float32(1.0 / 16384)
    return weighted.reshape(snapshots.shape), gram


def solution(mesh):
    parts = jax.sharding.Mesh(mesh.devices.reshape(4, 2, 2, 8, 2), ALL)
    along, side, snap = ("y", "xh"), "xl", ("z", "core")
    placed = (P(along, side, None, snap), P(along, side, None), P(along, side, None, None))
    return jax.shard_map(
        body,
        mesh=parts,
        in_specs=placed,
        out_specs=(P(along, side, None, snap), P(snap, PLANE)),
        check_vma=False,
    )
```

```python
import jax
import jax.numpy as jnp
from jax import lax
from jax.experimental import pallas as pl
from jax.experimental.pallas import tpu as pltpu
from jax.sharding import PartitionSpec as P

NEIGH = 9
BLK = 64
PLANE = ("y", "xh", "xl")
ALL = ("y", "xh", "xl", "z", "core")
SWAP = [(0, 1), (1, 0)]
UP = [(k, (k + 1) % 8) for k in range(8)]
DOWN = [(k, (k - 1) % 8) for k in range(8)]


def turned(z):
    return (z + 3) % 8 // 4 ^ 1


DOWN_TURNED = [
    (2 * k + c, 2 * ((k - 1) % 8) + (c ^ turned(k - 1))) for k in range(8) for c in range(2)
]
VMEM = pl.BlockSpec(memory_space=pltpu.VMEM)
SMEM = pl.BlockSpec(memory_space=pltpu.SMEM)
CORE, SIDE, ROW, COLUMN, OWN = range(5)


def split(value):
    high = value.astype(jnp.bfloat16)
    return high, (value - high.astype(jnp.float32)).astype(jnp.bfloat16)


def call(kernel, shape, scratch, scalars, *arrays, after=()):
    lead = len(scalars) + len(arrays)

    def ordered(*refs):
        kernel(*refs[:lead], *refs[lead + len(after) :])

    return pl.pallas_call(
        ordered,
        out_shape=shape,
        in_specs=[SMEM] * len(scalars)
        + [VMEM] * len(arrays)
        + [pl.BlockSpec(memory_space=pl.ANY)] * len(after),
        out_specs=jax.tree.map(lambda _: VMEM, shape),
        scratch_shapes=scratch,
        compiler_params=pltpu.CompilerParams(vmem_limit_bytes=40 * 1024 * 1024),
        cost_estimate=pl.CostEstimate(flops=1, bytes_accessed=1, transcendentals=0),
    )(*scalars, *arrays, *after)


def stencil(factors, highs, lows):
    first = lax.broadcasted_iota(jnp.int32, (32, 128), 1) < BLK
    highs, lows = list(highs), list(lows)
    evens, odds = [], []
    for k in range(0, len(factors), 2):
        left = factors[k]
        if k + 1 < len(factors):
            right = factors[k + 1]
        else:
            right = jnp.zeros((32, 128), jnp.float32)
            highs.append(highs[-1])
            lows.append(lows[-1])
        evens.append(jnp.where(first, left, pltpu.roll(right, BLK, 1)))
        odds.append(jnp.where(first, pltpu.roll(left, BLK, 1), right))
    lhs = jnp.concatenate([jnp.concatenate(evens, 1), jnp.concatenate(odds, 1)], 0)
    lhs_high, lhs_low = split(lhs)
    both = jnp.dot(
        jnp.concatenate([lhs_high, lhs_low], 0),
        jnp.concatenate(highs, 0),
        preferred_element_type=jnp.float32,
    )
    return both[:BLK] + (
        both[BLK:]
        + jnp.dot(lhs_high, jnp.concatenate(lows, 0), preferred_element_type=jnp.float32)
    )


def factor(mass, a, k, b):
    return mass[a, k, b : b + 1, :].reshape(32, 128)


def halves(count, cols):
    return [pltpu.VMEM((count, BLK, cols), jnp.bfloat16)] * 2


def weave(out, at, woven, value):
    for half in range(2):
        lanes = slice(half * 128, half * 128 + 128)
        woven[half, pl.ds(0, 32, stride=2), :] = value[:32, lanes]
        woven[half, pl.ds(1, 32, stride=2), :] = value[32:, lanes]
        out[at, :, lanes] = woven[half]


def side_terms(spot, places, mass, a, high, low):
    side = spot[SIDE]
    factors = []
    for shift in range(3):
        place = places[(a * 4 + 3 - 3 * side) * NEIGH + shift * 3 + 2 - 2 * side]
        factors.append(
            jnp.where(side == 0, factor(mass, a, place, 3), factor(mass, a, place, 0))
        )
    return stencil(
        factors, [high[a + shift] for shift in range(3)], [low[a + shift] for shift in range(3)]
    )


def weigh_mid(spot, places, own, y_side, mass, mid, outer, total, high, low, y_high, y_low, woven):
    for block in range(16):
        high[block], low[block] = split(own[block])
    for a in range(4):
        y_high[1 + a], y_low[1 + a] = split(y_side[a])
    for a in range(4):
        for b in range(4):
            factors, highs, lows = [], [], []
            for code in range(NEIGH):
                row, column = a + code // 3 - 1, b + code % 3 - 1
                if 0 <= row < 4 and 0 <= column < 4:
                    factors.append(factor(mass, a, places[(a * 4 + b) * NEIGH + code], b))
                    highs.append(high[row * 4 + column])
                    lows.append(low[row * 4 + column])
            value = stencil(factors, highs, lows)
            if a in (1, 2):
                total[a * 4 - 4 + b] = value
            else:
                outer[a // 3 * 4 + b] = value
    b = 3 - 3 * spot[SIDE]
    for a in (1, 2):
        at = a * 4 - 4 + b
        total[at] = total[at] + side_terms(spot, places, mass, a, y_high, y_low)
    for block in range(8):
        weave(mid, block, woven, total[block])


def weigh_outer(
    spot, places, part, x_low, x_high, y_side, corners, mass, mid, outer, out, total, high, low, y_high, y_low, woven
):
    for b in range(4):
        high[b], low[b] = split(x_low[b])
        high[4 + b], low[4 + b] = split(x_high[b])
        y_high[1 + b], y_low[1 + b] = split(y_side[b])
    y_high[0], y_low[0] = split(corners[0])
    y_high[5], y_low[5] = split(corners[1])
    for a, code_at, halo in ((0, 0, 0), (3, 6, 4)):
        for b in range(4):
            factors, highs, lows = [], [], []
            for shift in range(3):
                column = b + shift - 1
                if 0 <= column < 4:
                    place = places[(a * 4 + b) * NEIGH + code_at + shift]
                    factors.append(factor(mass, a, place, b))
                    highs.append(high[halo + column])
                    lows.append(low[halo + column])
            total[halo + b] = part[halo + b] + stencil(factors, highs, lows)
        at = halo + 3 - 3 * spot[SIDE]
        total[at] = total[at] + side_terms(spot, places, mass, a, y_high, y_low)
    for block in range(8):
        weave(outer, block, woven, total[block])
    out[:4] = outer[:4]
    out[4:12] = mid[...]
    out[12:] = outer[4:]


def weigh(spot, snapshots, links, mass):
    side = lax.axis_index("xl")
    edge = jnp.where(side == 0, snapshots[:, 3], snapshots[:, 0])
    along = ("y", "xh")
    y_side = lax.ppermute(edge, "xl", SWAP)
    x_low = lax.ppermute(snapshots[3], along, [(i, i + 1) for i in range(7)])
    x_high = lax.ppermute(snapshots[0], along, [(i + 1, i) for i in range(7)])
    cols = snapshots.shape[3]
    codes = jnp.arange(NEIGH, dtype=jnp.int32)
    places = jnp.sum(
        jnp.where(links.reshape(16, NEIGH, 1) == codes, codes[:, None], 0), axis=1
    ).reshape(-1)
    mass = mass.transpose(0, 2, 1, 3)

    def blocks(count):
        return jax.ShapeDtypeStruct((count, BLK, cols), jnp.float32)

    total, woven = pltpu.VMEM((8, BLK, cols), jnp.float32), pltpu.VMEM((2, BLK, 128), jnp.float32)
    mid, part = call(
        weigh_mid,
        [blocks(8)] * 2,
        [total] + halves(16, cols) + halves(6, cols) + [woven],
        [spot, places],
        snapshots.reshape(16, BLK, cols),
        y_side,
        mass,
    )
    flat = mid.reshape(8 * BLK, cols)
    early = [lax.ppermute(flat, "z", UP), lax.ppermute(flat, ("z", "core"), DOWN_TURNED)]
    x_low, x_high, mid = lax.optimization_barrier((x_low, x_high, mid))
    corners = jnp.where(
        side == 0, jnp.stack([x_low[3], x_high[3]]), jnp.stack([x_low[0], x_high[0]])
    )
    corners = lax.ppermute(corners, "xl", SWAP)
    outer, weighted = call(
        weigh_outer,
        [blocks(8), blocks(16)],
        [total] + halves(8, cols) + halves(6, cols) + [woven],
        [spot, places],
        part,
        x_low,
        x_high,
        y_side,
        corners,
        mass,
        mid,
    )
    outer, *early = lax.optimization_barrier((outer, *early))
    return flat, outer.reshape(8 * BLK, cols), weighted, early


def dot(left, right):
    def one(a, b):
        return lax.dot_general(a, b, (((0,), (0,)), ((), ())), preferred_element_type=jnp.float32)

    return one(left[0], right[0]) + (one(left[0], right[1]) + one(left[1], right[0]))


def whole(pair):
    parts = [split(ref[...]) for ref in pair]
    return tuple(jnp.concatenate([parts[0][k], parts[1][k]], 0) for k in range(2))


def columns(value, start, stop):
    return tuple(part[:, start:stop] for part in value)


def lay(out, at, block):
    for i in range(2):
        for j in range(2):
            out[at + 4 * i + j, :128, :] = block[i * 128 : i * 128 + 128, j * 128 : j * 128 + 128]


def square_kernel(spot, *refs):
    *arrays, square = refs
    own, other = whole(arrays[:2]), whole(arrays[2:])
    first = spot[CORE] == 0
    left = tuple(
        jnp.where(first, a, b) for a, b in zip(columns(own, 0, 128), columns(other, 128, 256))
    )
    right = tuple(jnp.where(first, a, b) for a, b in zip(other, own))
    cross = dot(left, right)
    square[...] = jnp.zeros(square.shape, jnp.float32)
    square[0, :128, :] = cross[:, :128]
    square[1, :128, :] = cross[:, 128:]
    diagonal = dot(own, own)
    row = lax.broadcasted_iota(jnp.int32, (128, 128), 0)
    column = lax.broadcasted_iota(jnp.int32, (128, 128), 1)
    low_end = diagonal[128:, 128:]
    square[2, :128, :] = jnp.where(row <= column, diagonal[:128, :128], low_end)
    square[2, 128:129, :] = jnp.sum(jnp.where(row == column, low_end, 0.0), 0, keepdims=True)
    square[3, :128, :] = diagonal[:128, 128:]


def near_products(mine, refs):
    held, beside, last, own = [split(ref[...]) for ref in refs]
    return (2 * mine, dot(own, held)), (2 * (1 - mine), dot(own, beside)), (8, dot(last, own))


def near_kernel(spot, *refs):
    *arrays, square, out = refs
    out[:, 128:, :] = jnp.zeros((16, 8, 128), jnp.float32)
    for at, block in near_products(spot[CORE], arrays):
        lay(out, at, block)
    out[10:12] = square[:2]
    out[14:16] = square[2:]


def more_kernel(spot, *refs):
    *arrays, part, out = refs
    out[...] = part[...]
    for at, block in near_products(spot[CORE], arrays):
        for i in range(2):
            for j in range(2):
                place = at + 4 * i + j
                piece = block[i * 128 : i * 128 + 128, j * 128 : j * 128 + 128]
                out[place, :128, :] = part[place, :128, :] + piece


def far_kernel(spot, *refs):
    *arrays, out = refs
    mine = spot[OWN]
    last_2, own, other, opposite, last_1 = [whole(arrays[k : k + 2]) for k in range(0, 10, 2)]
    lay(out, 2 * mine, dot(last_2, own))
    lay(out, 2 * (1 - mine), dot(last_2, other))
    lay(out, 8, dot(last_2, opposite))
    lay(out, 10, dot(last_1, other))


def add_kernel(blocks, out):
    total = blocks[0]
    for piece in range(1, 16):
        total = total + blocks[piece]
    out[...] = total


def send_kernel(spot, far, far_beside, near, near_beside, *outs):
    y, x, core = spot[ROW], spot[COLUMN], spot[CORE]
    beside = x % 2
    even = jnp.where(beside == 0, near[...], near_beside[...])
    odd = jnp.where(beside == 0, near_beside[...], near[...])[:128]
    row = lax.broadcasted_iota(jnp.int32, (128, 128), 0)
    column = lax.broadcasted_iota(jnp.int32, (128, 128), 1)
    packed = even[:128]
    upper = jnp.where(row <= column, packed, 0.0)
    upper = upper + jnp.where(row < column, packed, 0.0).T
    lower = jnp.where(row > column, packed, 0.0)
    lower = lower + lower.T + jnp.where(row == column, even[128:129], 0.0)
    diagonal = (y == 3) & (x >= 2)
    lefts = jnp.where(diagonal, jnp.where(beside == 0, upper, odd.T), packed)
    rights = jnp.where(diagonal & (beside == 1), lower, odd)
    far_left = jnp.where(beside == 0, far[...], far_beside[...])
    far_right = jnp.where(beside == 0, far_beside[...], far[...])
    late = (y + beside + core) % 2
    turned = (beside == 1) & jnp.logical_not(diagonal)
    lefts, rights = jnp.where(turned, lefts.T, lefts), jnp.where(turned, rights.T, rights)
    turned = beside == 1
    far_left = jnp.where(turned, far_left.T, far_left)
    far_right = jnp.where(turned, far_right.T, far_right)
    for turn in range(2):
        outs[turn][:, :128] = jnp.where(late == turn, far_left, lefts)
        outs[turn][:, 128:] = jnp.where(late == turn, far_right, rights)


def array(*shape):
    return jax.ShapeDtypeStruct(shape, jnp.float32)


def gathered(blocks):
    blocks = lax.all_to_all(blocks, PLANE, 0, 0, tiled=True)
    return call(add_kernel, array(*blocks.shape[1:]), [], [], blocks)


def crossed(z, core):
    return core if z % 8 < 4 else 1 - core


def routes(turn):
    pairs = []

    def flat(z, core, column):
        return (column % 16) * 16 + 2 * (z % 8) + core

    for i in range(4):
        for j in range(4):
            for z in range(8):
                for core in range(2):
                    late = turn == (i + j + core) % 2
                    mirror = j % 2 == 1
                    here = flat(z, core, 4 * i + j)
                    column = j // 2
                    row = core
                    if i < 2:
                        a, b = (z - 2, z + 1) if late else (z + 1, z)
                        row = core if late else core ^ turned(z)
                    elif j < 2 and late:
                        a, b, column = z - 2, z + 2, crossed(z, core)
                    elif j < 2 or late:
                        a, b, column = z - 1, z + 1, core ^ turned(z) ^ late
                    else:
                        a = b = z
                        row, column = (0, 1) if i == 2 else (core, core)
                        mirror = mirror and i == 2
                    there = flat(b, column, 2 * a + row) if mirror else flat(a, row, 2 * b + column)
                    pairs.append((here, there))
    return pairs


def body(snapshots, links, mass):
    y, x = lax.axis_index("y"), 2 * lax.axis_index("xh") + lax.axis_index("xl")
    z, core = lax.axis_index("z"), lax.axis_index("core")
    other = x % 2
    apart = ((4 * y + x) // 2 - z) % 8
    straight = other == jnp.where((z + 2) % 8 < 4, core, 1 - core)
    same = core == other
    after_same = other == core ^ turned(z + 1)
    before_same = core == other ^ turned(z + 7)
    mirror = (apart == 1) | (apart == 5) | (apart == 6)
    mirror = mirror | ((apart == 4) & jnp.logical_not(straight))
    mirror = mirror | ((apart == 0) & (core == 1) & (other == 0))
    turns = (
        jnp.where(same, core, 1 - core),
        other ^ turned(z),
        jnp.where(after_same, 1 - core, core),
        core,
        jnp.where(straight, core, 1 - other),
        1 - other,
        jnp.where(before_same, other, 1 - other),
        1 - core ^ turned(z + 7),
    )
    turn = sum(jnp.where(apart == k, value, 0) for k, value in enumerate(turns))
    spot = [core, lax.axis_index("xl"), y, x, core ^ turned(z)]
    spot = jnp.stack([jnp.asarray(value).astype(jnp.int32) for value in spot])
    *held, weighted, early = weigh(spot, snapshots, links, mass)
    next_1 = [early[1], lax.ppermute(held[1], ("z", "core"), DOWN_TURNED)]
    last_1 = [early[0], lax.ppermute(held[1], "z", UP)]
    held_other = [lax.ppermute(half, "core", SWAP) for half in held]
    square = call(square_kernel, array(4, 136, 128), [], [spot], *held, *held_other)
    sure = links[0, 0, 0] >= 0
    part = call(
        near_kernel,
        array(16, 136, 128),
        [],
        [spot],
        held[0],
        held_other[0],
        last_1[0],
        next_1[0],
        square,
    )
    next_1[1], part, sure = lax.optimization_barrier((next_1[1], part, sure))
    next_other = [lax.ppermute(half, "core", SWAP) for half in next_1]
    next_1[1], last_1[1], part, next_other[1] = lax.optimization_barrier(
        (next_1[1], last_1[1], part, next_other[1])
    )
    near = call(
        more_kernel,
        array(16, 136, 128),
        [],
        [spot],
        held[1],
        held_other[1],
        last_1[1],
        next_1[1],
        part,
    )
    next_1[1], last_1[1], near = lax.optimization_barrier((next_1[1], last_1[1], near))
    last_2 = [lax.ppermute(half, "z", UP) for half in last_1]
    next_2 = [lax.ppermute(half, "z", DOWN) for half in next_1]
    near = lax.cond(sure, gathered, lambda blocks: blocks[0], near)
    far = call(
        far_kernel,
        array(16, 128, 128),
        [],
        [spot],
        *last_2,
        *next_1,
        *next_other,
        *next_2,
        *last_1,
        after=(near,),
    )
    near_beside = lax.ppermute(near, "xl", SWAP)
    far = gathered(far)
    far_beside = lax.ppermute(far, "xl", SWAP)
    sent = call(
        send_kernel, [array(128, 256)] * 2, [], [spot], far, far_beside, near, near_beside
    )
    got = [lax.ppermute(sent[k], ALL, routes(k)) for k in range(2)]
    first = [jnp.where(turn == 0, got[0][:, k : k + 128], got[1][:, k : k + 128]) for k in (0, 128)]
    second = [jnp.where(turn == 0, got[1][:, k : k + 128], got[0][:, k : k + 128]) for k in (0, 128)]
    upper = jnp.concatenate([first[0], jnp.where(mirror, second[0], first[1])], 1)
    lower = jnp.concatenate([jnp.where(mirror, first[1], second[0]), second[1]], 1)
    gram = jnp.concatenate([upper, lower], 0) * jnp.float32(1.0 / 16384)
    return weighted.reshape(snapshots.shape), gram


def solution(mesh):
    parts = jax.sharding.Mesh(mesh.devices.reshape(4, 2, 2, 8, 2), ALL)
    along, side, snap = ("y", "xh"), "xl", ("z", "core")
    placed = (P(along, side, None, snap), P(along, side, None), P(along, side, None, None))
    return jax.shard_map(
        body,
        mesh=parts,
        in_specs=placed,
        out_specs=(P(along, side, None, snap), P(snap, PLANE)),
        check_vma=False,
    )
```

```python
import jax
import jax.numpy as jnp
from jax import lax
from jax.experimental import pallas as pl
from jax.experimental.pallas import tpu as pltpu
from jax.sharding import PartitionSpec as P

NEIGH = 9
BLK = 64
PLANE = ("y", "xh", "xl")
ALL = ("y", "xh", "xl", "z", "core")
SWAP = [(0, 1), (1, 0)]
UP = [(k, (k + 1) % 8) for k in range(8)]
DOWN = [(k, (k - 1) % 8) for k in range(8)]


def turned(z):
    return (z + 3) % 8 // 4 ^ 1


DOWN_TURNED = [
    (2 * k + c, 2 * ((k - 1) % 8) + (c ^ turned(k - 1))) for k in range(8) for c in range(2)
]
VMEM = pl.BlockSpec(memory_space=pltpu.VMEM)
SMEM = pl.BlockSpec(memory_space=pltpu.SMEM)
CORE, SIDE, ROW, COLUMN, OWN = range(5)


def split(value):
    high = value.astype(jnp.bfloat16)
    return high, (value - high.astype(jnp.float32)).astype(jnp.bfloat16)


def call(kernel, shape, scratch, scalars, *arrays, after=()):
    lead = len(scalars) + len(arrays)

    def ordered(*refs):
        kernel(*refs[:lead], *refs[lead + len(after) :])

    return pl.pallas_call(
        ordered,
        out_shape=shape,
        in_specs=[SMEM] * len(scalars)
        + [VMEM] * len(arrays)
        + [pl.BlockSpec(memory_space=pl.ANY)] * len(after),
        out_specs=jax.tree.map(lambda _: VMEM, shape),
        scratch_shapes=scratch,
        compiler_params=pltpu.CompilerParams(vmem_limit_bytes=40 * 1024 * 1024),
        cost_estimate=pl.CostEstimate(flops=1, bytes_accessed=1, transcendentals=0),
    )(*scalars, *arrays, *after)


def stencil(factors, highs, lows):
    first = lax.broadcasted_iota(jnp.int32, (32, 128), 1) < BLK
    highs, lows = list(highs), list(lows)
    evens, odds = [], []
    for k in range(0, len(factors), 2):
        left = factors[k]
        if k + 1 < len(factors):
            right = factors[k + 1]
        else:
            right = jnp.zeros((32, 128), jnp.float32)
            highs.append(highs[-1])
            lows.append(lows[-1])
        evens.append(jnp.where(first, left, pltpu.roll(right, BLK, 1)))
        odds.append(jnp.where(first, pltpu.roll(left, BLK, 1), right))
    lhs = jnp.concatenate([jnp.concatenate(evens, 1), jnp.concatenate(odds, 1)], 0)
    lhs_high, lhs_low = split(lhs)
    both = jnp.dot(
        jnp.concatenate([lhs_high, lhs_low], 0),
        jnp.concatenate(highs, 0),
        preferred_element_type=jnp.float32,
    )
    return both[:BLK] + (
        both[BLK:]
        + jnp.dot(lhs_high, jnp.concatenate(lows, 0), preferred_element_type=jnp.float32)
    )


def factor(mass, a, k, b):
    return mass[a, k, b : b + 1, :].reshape(32, 128)


def halves(count, cols):
    return [pltpu.VMEM((count, BLK, cols), jnp.bfloat16)] * 2


def weave(out, at, woven, value):
    for half in range(2):
        lanes = slice(half * 128, half * 128 + 128)
        woven[half, pl.ds(0, 32, stride=2), :] = value[:32, lanes]
        woven[half, pl.ds(1, 32, stride=2), :] = value[32:, lanes]
        out[at, :, lanes] = woven[half]


def side_terms(spot, places, mass, a, high, low):
    side = spot[SIDE]
    factors = []
    for shift in range(3):
        place = places[(a * 4 + 3 - 3 * side) * NEIGH + shift * 3 + 2 - 2 * side]
        factors.append(
            jnp.where(side == 0, factor(mass, a, place, 3), factor(mass, a, place, 0))
        )
    return stencil(
        factors, [high[a + shift] for shift in range(3)], [low[a + shift] for shift in range(3)]
    )


def weigh_mid(spot, places, own, y_side, mass, mid, outer, total, high, low, y_high, y_low, woven):
    for block in range(16):
        high[block], low[block] = split(own[block])
    for a in range(4):
        y_high[1 + a], y_low[1 + a] = split(y_side[a])
    for a in range(4):
        for b in range(4):
            factors, highs, lows = [], [], []
            for code in range(NEIGH):
                row, column = a + code // 3 - 1, b + code % 3 - 1
                if 0 <= row < 4 and 0 <= column < 4:
                    factors.append(factor(mass, a, places[(a * 4 + b) * NEIGH + code], b))
                    highs.append(high[row * 4 + column])
                    lows.append(low[row * 4 + column])
            value = stencil(factors, highs, lows)
            if a in (1, 2):
                total[a * 4 - 4 + b] = value
            else:
                outer[a // 3 * 4 + b] = value
    b = 3 - 3 * spot[SIDE]
    for a in (1, 2):
        at = a * 4 - 4 + b
        total[at] = total[at] + side_terms(spot, places, mass, a, y_high, y_low)
    for block in range(8):
        weave(mid, block, woven, total[block])


def weigh_outer(
    spot, places, part, x_low, x_high, y_side, corners, mass, mid, outer, out, total, high, low, y_high, y_low, woven
):
    for b in range(4):
        high[b], low[b] = split(x_low[b])
        high[4 + b], low[4 + b] = split(x_high[b])
        y_high[1 + b], y_low[1 + b] = split(y_side[b])
    y_high[0], y_low[0] = split(corners[0])
    y_high[5], y_low[5] = split(corners[1])
    for a, code_at, halo in ((0, 0, 0), (3, 6, 4)):
        for b in range(4):
            factors, highs, lows = [], [], []
            for shift in range(3):
                column = b + shift - 1
                if 0 <= column < 4:
                    place = places[(a * 4 + b) * NEIGH + code_at + shift]
                    factors.append(factor(mass, a, place, b))
                    highs.append(high[halo + column])
                    lows.append(low[halo + column])
            total[halo + b] = part[halo + b] + stencil(factors, highs, lows)
        at = halo + 3 - 3 * spot[SIDE]
        total[at] = total[at] + side_terms(spot, places, mass, a, y_high, y_low)
    for block in range(8):
        weave(outer, block, woven, total[block])
    out[:4] = outer[:4]
    out[4:12] = mid[...]
    out[12:] = outer[4:]


def weigh(spot, snapshots, links, mass):
    side = lax.axis_index("xl")
    edge = jnp.where(side == 0, snapshots[:, 3], snapshots[:, 0])
    along = ("y", "xh")
    y_side = lax.ppermute(edge, "xl", SWAP)
    x_low = lax.ppermute(snapshots[3], along, [(i, i + 1) for i in range(7)])
    x_high = lax.ppermute(snapshots[0], along, [(i + 1, i) for i in range(7)])
    cols = snapshots.shape[3]
    codes = jnp.arange(NEIGH, dtype=jnp.int32)
    places = jnp.sum(
        jnp.where(links.reshape(16, NEIGH, 1) == codes, codes[:, None], 0), axis=1
    ).reshape(-1)
    mass = mass.transpose(0, 2, 1, 3)

    def blocks(count):
        return jax.ShapeDtypeStruct((count, BLK, cols), jnp.float32)

    total, woven = pltpu.VMEM((8, BLK, cols), jnp.float32), pltpu.VMEM((2, BLK, 128), jnp.float32)
    mid, part = call(
        weigh_mid,
        [blocks(8)] * 2,
        [total] + halves(16, cols) + halves(6, cols) + [woven],
        [spot, places],
        snapshots.reshape(16, BLK, cols),
        y_side,
        mass,
    )
    flat = mid.reshape(8 * BLK, cols)
    early = [lax.ppermute(flat, "z", UP), lax.ppermute(flat, ("z", "core"), DOWN_TURNED)]
    x_low, x_high, mid = lax.optimization_barrier((x_low, x_high, mid))
    corners = jnp.where(
        side == 0, jnp.stack([x_low[3], x_high[3]]), jnp.stack([x_low[0], x_high[0]])
    )
    corners = lax.ppermute(corners, "xl", SWAP)
    outer, weighted = call(
        weigh_outer,
        [blocks(8), blocks(16)],
        [total] + halves(8, cols) + halves(6, cols) + [woven],
        [spot, places],
        part,
        x_low,
        x_high,
        y_side,
        corners,
        mass,
        mid,
    )
    outer, *early = lax.optimization_barrier((outer, *early))
    return flat, outer.reshape(8 * BLK, cols), weighted, early


def dot(left, right):
    def one(a, b):
        return lax.dot_general(a, b, (((0,), (0,)), ((), ())), preferred_element_type=jnp.float32)

    return one(left[0], right[0]) + (one(left[0], right[1]) + one(left[1], right[0]))


def dots(left, *rights):
    total = dot(left, tuple(jnp.concatenate(parts, 1) for parts in zip(*rights)))
    return [total[:, k * 256 : k * 256 + 256] for k in range(len(rights))]


def whole(pair):
    parts = [split(ref[...]) for ref in pair]
    return tuple(jnp.concatenate([parts[0][k], parts[1][k]], 0) for k in range(2))


def columns(value, start, stop):
    return tuple(part[:, start:stop] for part in value)


def lay(out, at, block):
    for i in range(2):
        for j in range(2):
            out[at + 4 * i + j, :128, :] = block[i * 128 : i * 128 + 128, j * 128 : j * 128 + 128]


def square_kernel(spot, *refs):
    *arrays, square = refs
    own, other = whole(arrays[:2]), whole(arrays[2:])
    first = spot[CORE] == 0
    left = tuple(
        jnp.where(first, a, b) for a, b in zip(columns(own, 0, 128), columns(other, 128, 256))
    )
    right = tuple(jnp.where(first, a, b) for a, b in zip(other, own))
    cross = dot(left, right)
    square[...] = jnp.zeros(square.shape, jnp.float32)
    square[0, :128, :] = cross[:, :128]
    square[1, :128, :] = cross[:, 128:]
    diagonal = dot(own, own)
    row = lax.broadcasted_iota(jnp.int32, (128, 128), 0)
    column = lax.broadcasted_iota(jnp.int32, (128, 128), 1)
    low_end = diagonal[128:, 128:]
    square[2, :128, :] = jnp.where(row <= column, diagonal[:128, :128], low_end)
    square[2, 128:129, :] = jnp.sum(jnp.where(row == column, low_end, 0.0), 0, keepdims=True)
    square[3, :128, :] = diagonal[:128, 128:]


def near_kernel(spot, *refs):
    *arrays, square, out = refs
    mine = spot[CORE]
    held, beside, last, own = [whole(arrays[k : k + 2]) for k in range(0, 8, 2)]
    out[:, 128:, :] = jnp.zeros((16, 8, 128), jnp.float32)
    same, cross = dots(own, held, beside)
    lay(out, 2 * mine, same)
    lay(out, 2 * (1 - mine), cross)
    lay(out, 8, dot(last, own))
    out[10:12] = square[:2]
    out[14:16] = square[2:]


def far_kernel(spot, *refs):
    *arrays, out = refs
    mine = spot[OWN]
    last_2, own, other, opposite, last_1 = [whole(arrays[k : k + 2]) for k in range(0, 10, 2)]
    same, cross, across = dots(last_2, own, other, opposite)
    lay(out, 2 * mine, same)
    lay(out, 2 * (1 - mine), cross)
    lay(out, 8, across)
    lay(out, 10, dot(last_1, other))


def add_kernel(blocks, out):
    total = blocks[0]
    for piece in range(1, 16):
        total = total + blocks[piece]
    out[...] = total


def send_kernel(spot, far, far_beside, near, near_beside, *outs):
    y, x, core = spot[ROW], spot[COLUMN], spot[CORE]
    beside = x % 2
    even = jnp.where(beside == 0, near[...], near_beside[...])
    odd = jnp.where(beside == 0, near_beside[...], near[...])[:128]
    row = lax.broadcasted_iota(jnp.int32, (128, 128), 0)
    column = lax.broadcasted_iota(jnp.int32, (128, 128), 1)
    packed = even[:128]
    upper = jnp.where(row <= column, packed, 0.0)
    upper = upper + jnp.where(row < column, packed, 0.0).T
    lower = jnp.where(row > column, packed, 0.0)
    lower = lower + lower.T + jnp.where(row == column, even[128:129], 0.0)
    diagonal = (y == 3) & (x >= 2)
    lefts = jnp.where(diagonal, jnp.where(beside == 0, upper, odd.T), packed)
    rights = jnp.where(diagonal & (beside == 1), lower, odd)
    far_left = jnp.where(beside == 0, far[...], far_beside[...])
    far_right = jnp.where(beside == 0, far_beside[...], far[...])
    late = (y + beside + core) % 2
    turned = (beside == 1) & jnp.logical_not(diagonal)
    lefts, rights = jnp.where(turned, lefts.T, lefts), jnp.where(turned, rights.T, rights)
    turned = beside == 1
    far_left = jnp.where(turned, far_left.T, far_left)
    far_right = jnp.where(turned, far_right.T, far_right)
    for turn in range(2):
        outs[turn][:, :128] = jnp.where(late == turn, far_left, lefts)
        outs[turn][:, 128:] = jnp.where(late == turn, far_right, rights)


def array(*shape):
    return jax.ShapeDtypeStruct(shape, jnp.float32)


def gathered(blocks):
    blocks = lax.all_to_all(blocks, PLANE, 0, 0, tiled=True)
    return call(add_kernel, array(*blocks.shape[1:]), [], [], blocks)


def crossed(z, core):
    return core if z % 8 < 4 else 1 - core


def routes(turn):
    pairs = []

    def flat(z, core, column):
        return (column % 16) * 16 + 2 * (z % 8) + core

    for i in range(4):
        for j in range(4):
            for z in range(8):
                for core in range(2):
                    late = turn == (i + j + core) % 2
                    mirror = j % 2 == 1
                    here = flat(z, core, 4 * i + j)
                    column = j // 2
                    row = core
                    if i < 2:
                        a, b = (z - 2, z + 1) if late else (z + 1, z)
                        row = core if late else core ^ turned(z)
                    elif j < 2 and late:
                        a, b, column = z - 2, z + 2, crossed(z, core)
                    elif j < 2 or late:
                        a, b, column = z - 1, z + 1, core ^ turned(z) ^ late
                    else:
                        a = b = z
                        row, column = (0, 1) if i == 2 else (core, core)
                        mirror = mirror and i == 2
                    there = flat(b, column, 2 * a + row) if mirror else flat(a, row, 2 * b + column)
                    pairs.append((here, there))
    return pairs


def body(snapshots, links, mass):
    y, x = lax.axis_index("y"), 2 * lax.axis_index("xh") + lax.axis_index("xl")
    z, core = lax.axis_index("z"), lax.axis_index("core")
    other = x % 2
    apart = ((4 * y + x) // 2 - z) % 8
    straight = other == jnp.where((z + 2) % 8 < 4, core, 1 - core)
    same = core == other
    after_same = other == core ^ turned(z + 1)
    before_same = core == other ^ turned(z + 7)
    mirror = (apart == 1) | (apart == 5) | (apart == 6)
    mirror = mirror | ((apart == 4) & jnp.logical_not(straight))
    mirror = mirror | ((apart == 0) & (core == 1) & (other == 0))
    turns = (
        jnp.where(same, core, 1 - core),
        other ^ turned(z),
        jnp.where(after_same, 1 - core, core),
        core,
        jnp.where(straight, core, 1 - other),
        1 - other,
        jnp.where(before_same, other, 1 - other),
        1 - core ^ turned(z + 7),
    )
    turn = sum(jnp.where(apart == k, value, 0) for k, value in enumerate(turns))
    spot = [core, lax.axis_index("xl"), y, x, core ^ turned(z)]
    spot = jnp.stack([jnp.asarray(value).astype(jnp.int32) for value in spot])
    *held, weighted, early = weigh(spot, snapshots, links, mass)
    next_1 = [early[1], lax.ppermute(held[1], ("z", "core"), DOWN_TURNED)]
    last_1 = [early[0], lax.ppermute(held[1], "z", UP)]
    held_other = [lax.ppermute(half, "core", SWAP) for half in held]
    square = call(square_kernel, array(4, 136, 128), [], [spot], *held, *held_other)
    sure = links[0, 0, 0] >= 0
    next_1[1], square, sure = lax.optimization_barrier((next_1[1], square, sure))
    next_other = [lax.ppermute(half, "core", SWAP) for half in next_1]
    next_1[1], last_1[1], square, next_other[1] = lax.optimization_barrier(
        (next_1[1], last_1[1], square, next_other[1])
    )
    near = call(
        near_kernel,
        array(16, 136, 128),
        [],
        [spot],
        *held,
        *held_other,
        *last_1,
        *next_1,
        square,
    )
    next_1[1], last_1[1], near = lax.optimization_barrier((next_1[1], last_1[1], near))
    last_2 = [lax.ppermute(half, "z", UP) for half in last_1]
    next_2 = [lax.ppermute(half, "z", DOWN) for half in next_1]
    near = lax.cond(sure, gathered, lambda blocks: blocks[0], near)
    far = call(
        far_kernel,
        array(16, 128, 128),
        [],
        [spot],
        *last_2,
        *next_1,
        *next_other,
        *next_2,
        *last_1,
        after=(near,),
    )
    near_beside = lax.ppermute(near, "xl", SWAP)
    far = gathered(far)
    far_beside = lax.ppermute(far, "xl", SWAP)
    sent = call(
        send_kernel, [array(128, 256)] * 2, [], [spot], far, far_beside, near, near_beside
    )
    got = [lax.ppermute(sent[k], ALL, routes(k)) for k in range(2)]
    first = [jnp.where(turn == 0, got[0][:, k : k + 128], got[1][:, k : k + 128]) for k in (0, 128)]
    second = [jnp.where(turn == 0, got[1][:, k : k + 128], got[0][:, k : k + 128]) for k in (0, 128)]
    upper = jnp.concatenate([first[0], jnp.where(mirror, second[0], first[1])], 1)
    lower = jnp.concatenate([jnp.where(mirror, first[1], second[0]), second[1]], 1)
    gram = jnp.concatenate([upper, lower], 0) * jnp.float32(1.0 / 16384)
    return weighted.reshape(snapshots.shape), gram


def solution(mesh):
    parts = jax.sharding.Mesh(mesh.devices.reshape(4, 2, 2, 8, 2), ALL)
    along, side, snap = ("y", "xh"), "xl", ("z", "core")
    placed = (P(along, side, None, snap), P(along, side, None), P(along, side, None, None))
    return jax.shard_map(
        body,
        mesh=parts,
        in_specs=placed,
        out_specs=(P(along, side, None, snap), P(snap, PLANE)),
        check_vma=False,
    )
```
